32 devices in a mesh: dom: 8 (over z, y), batch: 4 (over x, core).
Axes of the slice: x: 2, y: 2, z: 4, core: 2. Of those that a mesh axis runs over, the one named last changes fastest.
Arguments:
- activations: bfloat16 [1024, 65536], P('batch', 'dom'), may hold values from 0 to 2
- tile_weights: bfloat16 [4, 512, 512, 128], P(None, 'dom', 'batch'), may hold values from -0.375 to 0.375
- biases: float32 [4, 65536], P(None, 'dom'), may hold values from -2.5 to 2.5
- source_codes: int32 [4, 512, 4], P(None, 'dom'), may hold values from 0 to 67
- send_list: int32 [4, 8, 4], P(None, 'dom'), may hold values from 0 to 63
Outputs:
- result: bfloat16 [1024, 65536], P('batch', 'dom')
The draws below stay inside these ranges and needn't reach their ends.
All inputs are finite; a program needn't handle non-finite values.
Results may differ from the reference program's by a relative error of at most 0.0062.
Values may be sent and summed in bfloat16 or wider, within the bound.
No kernel may reach another device: no remote copies, remote signals or barrier semaphores. Data moves between devices by JAX's collectives and lax.ppermute only.
A program may use at most 192 MiB of HBM per device.

```python
import jax
import jax.numpy as jnp
from jax import lax

NEURONS = 65536
TILE = 128
FANIN = 4
NEIGH = 4
LAYERS = 4
ROWS = 1024
BLOCKS = 512
BLK_DEV = 64
PARTS_SIZE = 8


def plant(values, key, low, top_value):
    place = [jax.random.randint(jax.random.fold_in(key, axis), (), 0, length) for axis, length in enumerate(values.shape)]
    main_axis = values.shape.index(max(values.shape))
    beside = place[:main_axis] + [(place[main_axis] + 1) % values.shape[main_axis]] + place[main_axis + 1:]
    return values.at[tuple(place)].set(low).at[tuple(beside)].set(top_value)


def steps_of(rng, shape, shards, low, top_value):
    def one(dim, blocks):
        heights = jax.random.uniform(jax.random.fold_in(jax.random.fold_in(rng, 6), dim), (blocks,), jnp.float32, low / len(shards), top_value / len(shards))
        return jnp.repeat(jnp.exp(heights), shape[dim] // blocks).reshape((-1,) + (1,) * (len(shape) - dim - 1))

    factor_of = one(*shards[0])
    for cut in shards[1:]:
        factor_of = factor_of * one(*cut)
    return factor_of


def centred(rng, dims, spread, bound, cuts=(), dtype=jnp.bfloat16):
    factor_of = steps_of(rng, dims, cuts, -0.22, 0.18) if cuts else 1.0
    result = jax.random.normal(rng, dims, jnp.float32) * spread * factor_of
    return jnp.minimum(jnp.maximum(result, -bound), bound).astype(dtype)


def setup_inputs(seed: int = 0) -> dict:
    streams_of = jax.random.split(jax.random.key(seed), 6)
    activations = jnp.clip(2.0 * jax.random.uniform(streams_of[0], (ROWS, NEURONS), jnp.float32) ** steps_of(streams_of[0], (ROWS, NEURONS), ((0, 4), (1, 8)), -0.2, 0.2), 0.0, 2.0).astype(jnp.bfloat16)
    tile_weights = centred(streams_of[1], (LAYERS, BLOCKS, FANIN * TILE, TILE), (FANIN * TILE // 2) ** -0.5, 0.375, ((1, 8), (2, 4)))
    biases = centred(streams_of[2], (LAYERS, NEURONS), 0.5, 2.5, ((1, 8),), jnp.float32)
    source_codes = plant(jax.random.randint(streams_of[3], (LAYERS, BLOCKS, FANIN), 0, BLK_DEV + NEIGH), jax.random.fold_in(streams_of[3], 1), 0, (BLK_DEV + NEIGH) - 1).astype(jnp.int32)
    send_list = plant(jax.random.randint(streams_of[4], (LAYERS, PARTS_SIZE, NEIGH), 0, BLK_DEV), jax.random.fold_in(streams_of[4], 1), 0, BLK_DEV - 1).astype(jnp.int32)
    return dict(activations=activations, tile_weights=tile_weights, biases=biases, source_codes=source_codes, send_list=send_list)


def source_blocks(code_table, send_table):
    partition = (jnp.arange(BLOCKS) // BLK_DEV).astype(jnp.int32)[:, None]
    offset_table = jnp.array((1, 2, -1, PARTS_SIZE // 2), jnp.int32)
    slot_index = jnp.clip(code_table - BLK_DEV, 0, NEIGH - 1).astype(jnp.int32)
    sender_part = ((partition - offset_table[slot_index]) % PARTS_SIZE).astype(jnp.int32)
    remote_block = sender_part * BLK_DEV + send_table[sender_part, slot_index]
    local_block = partition * BLK_DEV + code_table
    return jnp.where(code_table < BLK_DEV, local_block, remote_block).astype(jnp.int32)


def reference(activations, tile_weights, biases, source_codes, send_list):
    current = activations
    group_count = BLOCKS // 16
    for layer_index in range(LAYERS):
        sources = source_blocks(source_codes[layer_index], send_list[layer_index])
        blocked = current.reshape(ROWS, BLOCKS, TILE)
        group_sources = sources.reshape(group_count, 16 * FANIN)
        group_tiles = tile_weights[layer_index].reshape(group_count, 16, FANIN * TILE, TILE)
        group_bias = biases[layer_index].reshape(group_count, 16, TILE)

        def one_group(pieces):
            index_row, weight_group, bias_group = pieces
            input_panel = jnp.take(blocked, index_row, axis=1).reshape(ROWS, 16, FANIN * TILE)
            summed = jnp.einsum("rjc,jco->rjo", input_panel.astype(jnp.float32), weight_group.astype(jnp.float32))
            return summed + bias_group[None].astype(jnp.float32)

        outputs = lax.map(one_group, (group_sources, group_tiles, group_bias))
        outputs = jnp.transpose(outputs, (1, 0, 2, 3)).reshape(ROWS, NEURONS)
        current = jnp.maximum(outputs, 0.0).astype(jnp.bfloat16)
    return current
```

```python
import functools

import jax
import jax.numpy as jnp
from jax import lax
from jax.experimental import pallas as pl
from jax.experimental.pallas import tpu as pltpu
from jax.sharding import PartitionSpec as P


def shifted(block, axis, distance):
    devices = range(lax.axis_size(axis))
    route = [((i - distance) % len(devices), i) for i in devices]
    return lax.ppermute(block, axis, route)


def swapped(block, mask):
    route = [(i, i ^ mask) for i in range(lax.axis_size("batch"))]
    return lax.ppermute(block, "batch", route)


def layer_kernel(layer, first, group, blocks, fan, neigh, width, aliased, *refs):
    codes, own = refs[:2]
    refs = refs[2:]
    current, arrived, tiles = refs[0], refs[1 : 1 + neigh], refs[1 + neigh : 1 + neigh + fan]
    refs = refs[1 + neigh + fan :]
    bias = refs[0]
    result, pool, semaphores = refs[2:] if aliased else refs[1:]
    step = pl.program_id(0)

    @pl.when(step == 0)
    def _():
        copies = [pltpu.make_async_copy(current, pool.at[:, : blocks * width], semaphores.at[neigh])]
        for slot in range(neigh):
            place = pl.ds((blocks + slot) * width, width)
            copies.append(pltpu.make_async_copy(arrived[slot], pool.at[:, place], semaphores.at[slot]))
        for copy in copies:
            copy.start()
        for copy in copies:
            copy.wait()

    for g in range(group):
        base = (layer * blocks + first + step * group + g) * fan
        panel = []
        for m in range(fan):
            code = codes[base + (own[0] ^ m)]
            panel.append(pool[:, pl.ds(pl.multiple_of(code * width, width), width)])
        summed = jnp.dot(
            jnp.concatenate(panel, axis=1),
            jnp.concatenate([tile[g] for tile in tiles], axis=0),
            preferred_element_type=jnp.float32,
        )
        columns = slice(g * width, (g + 1) * width)
        summed = summed + bias[layer : layer + 1, columns]
        result[:, columns] = jnp.maximum(summed, 0.0).astype(result.dtype)


def run_blocks(layer, first, count, codes, own, current, arrived, tiles, biases, target):
    rows, neurons = current.shape
    fan, neigh = len(tiles), len(arrived)
    width = tiles[0].shape[2]
    blocks = neurons // width
    group = min(8, count)
    steps = count // group
    offset = first // group
    anywhere = pl.BlockSpec(memory_space=pl.ANY)
    in_specs = [anywhere] * (1 + neigh)
    in_specs += [pl.BlockSpec((group, width, width), lambda i, *_: (i, 0, 0))] * fan
    in_specs += [pl.BlockSpec((biases.shape[0], group * width), lambda i, *_: (0, offset + i))]
    operands = [codes, own, current, *arrived, *tiles, biases]
    aliases = {}
    if target is not None:
        in_specs += [anywhere]
        aliases = {len(operands): 0}
        operands += [target]
    kernel = functools.partial(layer_kernel, layer, first, group, blocks, fan, neigh, width, target is not None)
    return pl.pallas_call(
        kernel,
        out_shape=jax.ShapeDtypeStruct((rows, neurons), current.dtype),
        grid_spec=pltpu.PrefetchScalarGridSpec(
            num_scalar_prefetch=2,
            grid=(steps,),
            in_specs=in_specs,
            out_specs=pl.BlockSpec((rows, group * width), lambda i, *_: (0, offset + i)),
            scratch_shapes=[
                pltpu.VMEM((rows, neurons + neigh * width), current.dtype),
                pltpu.SemaphoreType.DMA((neigh + 1,)),
            ],
        ),
        input_output_aliases=aliases,
        compiler_params=pltpu.CompilerParams(vmem_limit_bytes=40 * 2**20),
        cost_estimate=pl.CostEstimate(
            flops=2 * rows * count * fan * width * width,
            bytes_accessed=2 * (rows * neurons + rows * count * width + count * fan * width * width),
            transcendentals=0,
        ),
    )(*operands)


def body(activations, tile_weights, biases, source_codes, send_list):
    layer_count, block_count, part_rows, width = tile_weights.shape
    fan = source_codes.shape[2]
    part_count = lax.axis_size("dom")
    neighbor_offsets = (1, 2, -1, part_count // 2)
    sharers = width // part_rows
    own = (lax.axis_index("batch") // sharers).reshape(1).astype(jnp.int32)
    codes = source_codes.reshape(-1)
    far = fan // 2

    def local(layer, first, count):
        part = lax.slice(tile_weights, (layer, first, 0, 0), (layer + 1, first + count, part_rows, width))[0]
        if sharers == 1:
            return part
        members = range(lax.axis_size("batch") // sharers)
        groups = [[m * sharers + s for s in range(sharers)] for m in members]
        return lax.all_gather(part, "batch", axis=1, tiled=True, axis_index_groups=groups)

    chunks = [(layer, 0, block_count) for layer in range(layer_count - 1)]
    quarter = block_count // 4
    chunks += [(layer_count - 1, i * quarter, quarter) for i in range(4)]

    in_flight = 2
    sent, ready = [], []
    for index, chunk in enumerate(chunks):
        mine = local(*chunk)
        if index >= in_flight:
            mine, sent[index - in_flight] = lax.optimization_barrier((mine, sent[index - in_flight]))
        crossed = swapped(mine, far * sharers)
        sent.append(crossed)
        ready.append(mine)

    def tiles_of(index):
        held = [ready[index]] + [None] * (fan - 1)
        held[far] = sent[index]
        for bit in range(far.bit_length() - 1):
            for m in range(1 << bit):
                for start in (0, far):
                    held[start + m + (1 << bit)] = swapped(held[start + m], (1 << bit) * sharers)
        return held

    current = activations
    target = None
    for index, (layer, first, count) in enumerate(chunks):
        if first == 0:
            arrived = []
            for slot, offset in enumerate(neighbor_offsets):
                start = send_list[layer, 0, slot] * width
                block = lax.dynamic_slice(current, (0, start), (current.shape[0], width))
                arrived.append(shifted(block, "dom", offset))
            source, target = current, None
        current = target = run_blocks(
            layer, first, count, codes, own, source, arrived, tiles_of(index), biases, target
        )
    return current


def solution(mesh):
    in_specs = (
        P("batch", "dom"),
        P(None, "dom", "batch", None),
        P(None, "dom"),
        P(None, "dom", None),
        P(None, "dom", None),
    )
    out_specs = P("batch", "dom")
    return jax.shard_map(body, mesh=mesh, in_specs=in_specs, out_specs=out_specs, check_vma=False)
```

```python
import functools
import math

import jax
import jax.numpy as jnp
from jax import lax
from jax.experimental import pallas as pl
from jax.experimental.pallas import tpu as pltpu
from jax.sharding import PartitionSpec as P


PIECES = 4
FREE = pl.CostEstimate(flops=0, bytes_accessed=0, transcendentals=0)


def shifted(block, axis, distance):
    devices = range(lax.axis_size(axis))
    route = [((i - distance) % len(devices), i) for i in devices]
    return lax.ppermute(block, axis, route)


def swapped(block, mask):
    route = [(i, i ^ mask) for i in range(lax.axis_size("batch"))]
    return lax.ppermute(block, "batch", route)


def cut(tile_weights, layer, first, count, after):
    part = (count, *tile_weights.shape[2:])
    anywhere, in_hbm = (pl.BlockSpec(memory_space=space) for space in (pl.ANY, pltpu.HBM))

    def kernel(tiles, *refs):
        target, semaphore = refs[len(after) :]
        copy = pltpu.make_async_copy(tiles.at[layer, pl.ds(first, count)], target, semaphore)
        copy.start()
        copy.wait()

    return pl.pallas_call(
        kernel,
        out_shape=jax.ShapeDtypeStruct(part, tile_weights.dtype),
        in_specs=[in_hbm] + [anywhere] * len(after),
        out_specs=in_hbm,
        scratch_shapes=[pltpu.SemaphoreType.DMA],
        compiler_params=pltpu.CompilerParams(vmem_limit_bytes=56 * 2**20),
        cost_estimate=FREE,
    )(tile_weights, *after)


def layer_kernel(layer, first, group, blocks, neigh, width, pieces, aliased, *refs):
    refs = list(refs)
    codes, own, current = (refs.pop(0) for _ in range(3))
    arrived = [refs.pop(0) for _ in range(neigh)]
    tiles = [[refs.pop(0) for _ in range(number)] for number in pieces]
    bias = refs.pop(0)
    if aliased:
        refs.pop(0)
    result, pool, semaphores = refs
    fan = len(pieces)
    step = pl.program_id(0)

    @pl.when(step == 0)
    def _():
        copies = [pltpu.make_async_copy(current, pool.at[:, : blocks * width], semaphores.at[neigh])]
        for slot in range(neigh):
            place = pl.ds((blocks + slot) * width, width)
            copies.append(pltpu.make_async_copy(arrived[slot], pool.at[:, place], semaphores.at[slot]))
        for copy in copies:
            copy.start()
        for copy in copies:
            copy.wait()

    def work(held):
        for g in range(group):
            base = (layer * blocks + first + step * group + g) * fan
            panel = []
            for m in range(fan):
                code = codes[base + (own[0] ^ m)]
                panel.append(pool[:, pl.ds(pl.multiple_of(code * width, width), width)])
            summed = jnp.dot(
                jnp.concatenate(panel, axis=1),
                jnp.concatenate([tile[g] for tile in held], axis=0),
                preferred_element_type=jnp.float32,
            )
            columns = slice(g * width, (g + 1) * width)
            summed = summed + bias[layer : layer + 1, columns]
            result[:, columns] = jnp.maximum(summed, 0.0).astype(result.dtype)

    most = max(pieces)
    span = pl.num_programs(0) // most
    for part in range(most):

        @pl.when(step // span == part)
        def _():
            work([held[part * len(held) // most] for held in tiles])


def run_blocks(layer, first, count, codes, own, current, arrived, tiles, biases, target):
    rows, neurons = current.shape
    neigh, width = len(arrived), tiles[0].shape[3]
    blocks = neurons // width
    group = math.gcd(8, count // max(len(source) for source in tiles if isinstance(source, list)))
    steps = count // group
    offset = first // group
    anywhere = pl.BlockSpec(memory_space=pl.ANY)
    in_specs = [anywhere] * (1 + neigh)
    pieces, held = [], []
    for source in tiles:
        if isinstance(source, list):
            pieces.append(len(source))
            share = steps // len(source)
            for part, array in enumerate(source):
                held.append(array)
                in_specs.append(
                    pl.BlockSpec(
                        (group, width, width),
                        lambda i, *_, start=part * share, share=share: (jnp.clip(i - start, 0, share - 1), 0, 0),
                    )
                )
        else:
            pieces.append(1)
            held.append(source)
            in_specs.append(pl.BlockSpec((None, group, width, width), lambda i, *_: (layer, offset + i, 0, 0)))
    in_specs += [pl.BlockSpec((biases.shape[0], group * width), lambda i, *_: (0, offset + i))]
    operands = [codes, own, current, *arrived, *held, biases]
    aliases = {}
    if target is not None:
        in_specs += [anywhere]
        aliases = {len(operands): 0}
        operands += [target]
    kernel = functools.partial(layer_kernel, layer, first, group, blocks, neigh, width, pieces, target is not None)
    return pl.pallas_call(
        kernel,
        out_shape=jax.ShapeDtypeStruct((rows, neurons), current.dtype),
        grid_spec=pltpu.PrefetchScalarGridSpec(
            num_scalar_prefetch=2,
            grid=(steps,),
            in_specs=in_specs,
            out_specs=pl.BlockSpec((rows, group * width), lambda i, *_: (0, offset + i)),
            scratch_shapes=[
                pltpu.VMEM((rows, neurons + neigh * width), current.dtype),
                pltpu.SemaphoreType.DMA((neigh + 1,)),
            ],
        ),
        input_output_aliases=aliases,
        compiler_params=pltpu.CompilerParams(vmem_limit_bytes=52 * 2**20),
        cost_estimate=FREE,
    )(*operands)


def body(activations, tile_weights, biases, source_codes, send_list):
    layer_count, block_count, part_rows, width = tile_weights.shape
    fan = source_codes.shape[2]
    part_count = lax.axis_size("dom")
    neighbor_offsets = (1, 2, -1, part_count // 2)
    sharers = width // part_rows
    own = (lax.axis_index("batch") // sharers).reshape(1).astype(jnp.int32)
    codes = source_codes.reshape(-1)
    far = fan // 2
    unit = block_count // 16

    if sharers > 1:
        members = range(lax.axis_size("batch") // sharers)
        groups = [[m * sharers + s for s in range(sharers)] for m in members]
        tile_weights = lax.all_gather(tile_weights, "batch", axis=2, tiled=True, axis_index_groups=groups)

    def spread(held, first):
        for bit in range(far.bit_length() - 1):
            for m in range(1 << bit):
                held[first + m + (1 << bit)] = jax.tree.map(
                    lambda array: swapped(array, (1 << bit) * sharers), held[first + m]
                )

    last = layer_count - 1
    chunks = [(layer, 0, 16, PIECES) for layer in range(last)]
    chunks += [(last, 0, 8, PIECES), (last, 8, 4, PIECES), (last, 12, 4, 1)]
    chunks = [(layer, first * unit, count * unit, math.gcd(pieces, count * unit)) for layer, first, count, pieces in chunks]

    mine, crossed = {}, {}

    def send(index, *after):
        mine[index] = cut(tile_weights, *chunks[index][:3], after)
        crossed[index] = swapped(mine[index], far * sharers)

    near = [tile_weights] + [None] * (fan - 1)
    spread(near, 0)

    def tiles_of(index, *after):
        held = list(near)
        count, pieces = chunks[index][2:]
        arrived = lax.optimization_barrier((crossed[index], *after))[0]
        held[far] = [arrived[i * count // pieces : (i + 1) * count // pieces] for i in range(pieces)]
        spread(held, far)
        held[far] = [arrived]
        return held

    for index in range(len(chunks)):
        send(index)
    current = activations
    target = None
    for index, (layer, first, count, _) in enumerate(chunks):
        if first == 0:
            arrived = []
            for slot, offset in enumerate(neighbor_offsets):
                start = send_list[layer, 0, slot] * width
                block = lax.dynamic_slice(current, (0, start), (current.shape[0], width))
                arrived.append(shifted(block, "dom", offset))
            source, target = current, None
        before = [current] if index else []
        current = target = run_blocks(
            layer, first, count, codes, own, source, arrived, tiles_of(index, *before), biases, target
        )
    return current


def solution(mesh):
    in_specs = (
        P("batch", "dom"),
        P(None, "dom", "batch", None),
        P(None, "dom"),
        P(None, "dom", None),
        P(None, "dom", None),
    )
    out_specs = P("batch", "dom")
    return jax.shard_map(body, mesh=mesh, in_specs=in_specs, out_specs=out_specs, check_vma=False)
```

```python
import functools
import math

import jax
import jax.numpy as jnp
from jax import lax
from jax.experimental import pallas as pl
from jax.experimental.pallas import tpu as pltpu
from jax.sharding import PartitionSpec as P


PIECES = 4
FREE = pl.CostEstimate(flops=0, bytes_accessed=0, transcendentals=0)


def shifted(block, axis, distance):
    devices = range(lax.axis_size(axis))
    route = [((i - distance) % len(devices), i) for i in devices]
    return lax.ppermute(block, axis, route)


def swapped(block, mask):
    route = [(i, i ^ mask) for i in range(lax.axis_size("batch"))]
    return lax.ppermute(block, "batch", route)


def cut(tile_weights, layer, first, count):
    height, width = tile_weights.shape[2:]
    group = math.gcd(8, count)
    offset = first // group

    def kernel(tiles, target):
        target[...] = tiles[...]

    return pl.pallas_call(
        kernel,
        out_shape=jax.ShapeDtypeStruct((count, height, width), tile_weights.dtype),
        grid=(count // group,),
        in_specs=[pl.BlockSpec((None, group, height, width), lambda i: (layer, offset + i, 0, 0))],
        out_specs=pl.BlockSpec((group, height, width), lambda i: (i, 0, 0)),
        compiler_params=pltpu.CompilerParams(vmem_limit_bytes=52 * 2**20),
        cost_estimate=FREE,
    )(tile_weights)


def layer_kernel(layer, first, group, steps, blocks, neigh, width, pieces, aliased, *refs):
    refs = list(refs)
    codes, own, current = (refs.pop(0) for _ in range(3))
    arrived = [refs.pop(0) for _ in range(neigh)]
    tiles = [[refs.pop(0) for _ in range(number)] for number in pieces]
    bias = refs.pop(0)
    if aliased:
        refs.pop(0)
    result, pool, semaphores = refs
    fan = len(pieces)
    step = pl.program_id(0)

    @pl.when(step == 0)
    def _():
        copies = [pltpu.make_async_copy(current, pool.at[:, : blocks * width], semaphores.at[neigh])]
        for slot in range(neigh):
            place = pl.ds((blocks + slot) * width, width)
            copies.append(pltpu.make_async_copy(arrived[slot], pool.at[:, place], semaphores.at[slot]))
        for copy in copies:
            copy.start()
        for copy in copies:
            copy.wait()

    def tile(held, part, g):
        share = steps * group // len(held)
        if share >= group:
            return held[part * len(held) // parts][g]
        place = part * group + g
        return held[place // share][place % share]

    parts = min(max(pieces), steps)
    for part in range(parts):

        @pl.when(step // (steps // parts) == part)
        def _():
            for g in range(group):
                base = (layer * blocks + first + step * group + g) * fan
                panel = []
                for m in range(fan):
                    code = codes[base + (own[0] ^ m)]
                    panel.append(pool[:, pl.ds(pl.multiple_of(code * width, width), width)])
                summed = jnp.dot(
                    jnp.concatenate(panel, axis=1),
                    jnp.concatenate([tile(held, part, g) for held in tiles], axis=0),
                    preferred_element_type=jnp.float32,
                )
                columns = slice(g * width, (g + 1) * width)
                summed = summed + bias[layer : layer + 1, columns]
                result[:, columns] = jnp.maximum(summed, 0.0).astype(result.dtype)


def tile_spec(group, start, steps, width):
    return pl.BlockSpec((group, width, width), lambda i, *_: (jnp.clip(i - start, 0, steps - 1), 0, 0))


def run_blocks(layer, first, count, codes, own, current, arrived, tiles, biases, target):
    rows, neurons = current.shape
    neigh, width = len(arrived), tiles[0].shape[3]
    blocks = neurons // width
    group = math.gcd(8, count)
    steps = count // group
    offset = first // group
    anywhere = pl.BlockSpec(memory_space=pl.ANY)
    in_specs = [anywhere] * (1 + neigh)
    pieces, held = [], []
    for source in tiles:
        if isinstance(source, list):
            pieces.append(len(source))
            share = count // len(source)
            for part, array in enumerate(source):
                held.append(array)
                in_specs.append(tile_spec(min(group, share), part * share // group, max(1, share // group), width))
        else:
            pieces.append(1)
            held.append(source)
            in_specs.append(pl.BlockSpec((None, group, width, width), lambda i, *_: (layer, offset + i, 0, 0)))
    in_specs += [pl.BlockSpec((biases.shape[0], group * width), lambda i, *_: (0, offset + i))]
    operands = [codes, own, current, *arrived, *held, biases]
    aliases = {}
    if target is not None:
        in_specs += [anywhere]
        aliases = {len(operands): 0}
        operands += [target]
    kernel = functools.partial(layer_kernel, layer, first, group, steps, blocks, neigh, width, pieces, target is not None)
    return pl.pallas_call(
        kernel,
        out_shape=jax.ShapeDtypeStruct((rows, neurons), current.dtype),
        grid_spec=pltpu.PrefetchScalarGridSpec(
            num_scalar_prefetch=2,
            grid=(steps,),
            in_specs=in_specs,
            out_specs=pl.BlockSpec((rows, group * width), lambda i, *_: (0, offset + i)),
            scratch_shapes=[
                pltpu.VMEM((rows, neurons + neigh * width), current.dtype),
                pltpu.SemaphoreType.DMA((neigh + 1,)),
            ],
        ),
        input_output_aliases=aliases,
        compiler_params=pltpu.CompilerParams(vmem_limit_bytes=52 * 2**20),
        cost_estimate=FREE,
    )(*operands)


def body(activations, tile_weights, biases, source_codes, send_list):
    layer_count, block_count, part_rows, width = tile_weights.shape
    fan = source_codes.shape[2]
    part_count = lax.axis_size("dom")
    neighbor_offsets = (1, 2, -1, part_count // 2)
    sharers = width // part_rows
    own = (lax.axis_index("batch") // sharers).reshape(1).astype(jnp.int32)
    codes = source_codes.reshape(-1)
    far = fan // 2
    unit = block_count // 16

    if sharers > 1:
        members = range(lax.axis_size("batch") // sharers)
        groups = [[m * sharers + s for s in range(sharers)] for m in members]
        tile_weights = lax.all_gather(tile_weights, "batch", axis=2, tiled=True, axis_index_groups=groups)

    def spread(held, first):
        for bit in range(far.bit_length() - 1):
            for m in range(1 << bit):
                held[first + m + (1 << bit)] = jax.tree.map(
                    lambda array: swapped(array, (1 << bit) * sharers), held[first + m]
                )

    last = layer_count - 1
    chunks = [(layer, 0, 16, PIECES) for layer in range(last)]
    chunks += [(last, 0, 8, PIECES), (last, 8, 4, PIECES), (last, 12, 2, PIECES), (last, 14, 2, 1)]
    chunks = [(layer, first * unit, count * unit, math.gcd(pieces, count * unit)) for layer, first, count, pieces in chunks]

    mine, crossed = {}, {}

    def send(index):
        mine[index] = cut(tile_weights, *chunks[index][:3])
        crossed[index] = swapped(mine[index], far * sharers)

    near = [tile_weights] + [None] * (fan - 1)
    spread(near, 0)

    def tiles_of(index, *after):
        held = list(near)
        count, pieces = chunks[index][2:]
        arrived = lax.optimization_barrier((crossed[index], *after))[0]
        held[far] = [arrived[i * count // pieces : (i + 1) * count // pieces] for i in range(pieces)]
        spread(held, far)
        held[far] = [arrived]
        return held

    for index in range(len(chunks)):
        send(index)
    current = activations
    target = None
    for index, (layer, first, count, _) in enumerate(chunks):
        if first == 0:
            arrived = []
            for slot, offset in enumerate(neighbor_offsets):
                start = send_list[layer, 0, slot] * width
                block = lax.dynamic_slice(current, (0, start), (current.shape[0], width))
                arrived.append(shifted(block, "dom", offset))
            source, target = current, None
        before = [current] if index else []
        current = target = run_blocks(
            layer, first, count, codes, own, source, arrived, tiles_of(index, *before), biases, target
        )
    return current


def solution(mesh):
    in_specs = (
        P("batch", "dom"),
        P(None, "dom", "batch", None),
        P(None, "dom"),
        P(None, "dom", None),
        P(None, "dom", None),
    )
    out_specs = P("batch", "dom")
    return jax.shard_map(body, mesh=mesh, in_specs=in_specs, out_specs=out_specs, check_vma=False)
```

```python
import math

import jax
import jax.numpy as jnp
from jax import lax
from jax.experimental import pallas as pl
from jax.experimental.pallas import tpu as pltpu
from jax.sharding import PartitionSpec as P


PIECES = 4
VMEM_LIMIT = 52 * 2**20
FREE = pl.CostEstimate(flops=0, bytes_accessed=0, transcendentals=0)


def shifted(block, axis, distance):
    devices = range(lax.axis_size(axis))
    route = [((i - distance) % len(devices), i) for i in devices]
    return lax.ppermute(block, axis, route)


def swapped(block, mask):
    route = [(i, i ^ mask) for i in range(lax.axis_size("batch"))]
    return lax.ppermute(block, "batch", route)


def cut(tile_weights, chunks):
    height, width = tile_weights.shape[2:]
    moves = []
    for place, (layer, first, count) in enumerate(chunks):
        step = math.gcd(8, count)
        moves += [(place, layer, first, start, step) for start in range(0, count, step)]

    def kernel(tiles, *refs):
        targets, (room, arrive, leave) = refs[: len(chunks)], refs[len(chunks) :]
        inward, outward = [], []
        for index, (place, layer, first, start, step) in enumerate(moves):
            here = room.at[index, pl.ds(0, step)]
            source = tiles.at[layer, pl.ds(first + start, step)]
            inward.append(pltpu.make_async_copy(source, here, arrive.at[index]))
            outward.append(pltpu.make_async_copy(here, targets[place].at[pl.ds(start, step)], leave.at[index]))
        for copy in inward:
            copy.start()
        for before, after in zip(inward, outward):
            before.wait()
            after.start()
        for copy in outward:
            copy.wait()

    anywhere = pl.BlockSpec(memory_space=pl.ANY)
    return pl.pallas_call(
        kernel,
        out_shape=[jax.ShapeDtypeStruct((count, height, width), tile_weights.dtype) for _, _, count in chunks],
        in_specs=[anywhere],
        out_specs=[anywhere] * len(chunks),
        scratch_shapes=[
            pltpu.VMEM((len(moves), 8, height, width), tile_weights.dtype),
            pltpu.SemaphoreType.DMA((len(moves),)),
            pltpu.SemaphoreType.DMA((len(moves),)),
        ],
        compiler_params=pltpu.CompilerParams(vmem_limit_bytes=VMEM_LIMIT),
        cost_estimate=FREE,
    )(tile_weights)


def run_blocks(layer, first, count, codes, own, pool, arrived, tiles, biases, target, keep, final):
    fan, width = len(tiles), biases.shape[1] // (codes.shape[0] // (biases.shape[0] * len(tiles)))
    blocks = biases.shape[1] // width
    neigh = len(arrived) if arrived else pool.shape[0] - blocks
    rows = pool.shape[-2]
    gather = not arrived
    columns = pool.ndim == 2
    group = math.gcd(8, count)
    pieces = [len(source) if isinstance(source, list) else 1 for source in tiles]
    step = min(group, count // max(pieces))
    held = [source if isinstance(source, list) else [source] for source in tiles]

    def kernel(*refs):
        refs = list(refs)
        codes, own, pool_ref = (refs.pop(0) for _ in range(3))
        arrived_refs = [refs.pop(0) for _ in arrived]
        tile_refs = [[refs.pop(0) for _ in source] for source in held]
        bias = refs.pop(0)
        if target is not None:
            refs.pop(0)
        result = refs.pop(0)
        kept = refs.pop(0) if keep else None
        inputs, weights, outputs, in_sems, weight_sems, out_sems, keep_sem = refs

        def code_of(block, m):
            return codes[(layer * blocks + first + block) * fan + (own[0] ^ m)]

        def gathered(block, m):
            place = block * fan + m
            return pltpu.make_async_copy(pool_ref.at[code_of(block, m)], inputs.at[place], in_sems.at[place])

        def tile_copy(part, m):
            source = tile_refs[m]
            start = part * step
            if held[m][0].ndim == 4:
                piece = source[0].at[layer, pl.ds(first + start, step)]
            else:
                share = count // len(source)
                piece = source[start // share].at[pl.ds(start % share, step)]
            return pltpu.make_async_copy(piece, weights.at[m, pl.ds(start, step)], weight_sems.at[part, m])

        def out_copy(part):
            start = part * group
            if final:
                here = outputs.at[:, pl.ds(start * width, group * width)]
                there = result.at[:, pl.ds((first + start) * width, group * width)]
            else:
                here = outputs.at[pl.ds(start, group)]
                there = result.at[pl.ds(first + start, group)]
            return pltpu.make_async_copy(here, there, out_sems.at[part])

        loads = []
        if not gather:
            if columns:
                for block in range(blocks):
                    source = pool_ref.at[:, pl.ds(block * width, width)]
                    loads.append(pltpu.make_async_copy(source, inputs.at[block], in_sems.at[block]))
            else:
                half = blocks // 2
                for part in range(2):
                    source = pool_ref.at[pl.ds(part * half, half)]
                    loads.append(pltpu.make_async_copy(source, inputs.at[pl.ds(part * half, half)], in_sems.at[part]))
            for slot, source in enumerate(arrived_refs):
                loads.append(pltpu.make_async_copy(source, inputs.at[blocks + slot], in_sems.at[blocks + slot]))
            for copy in loads:
                copy.start()
        for part in range(count // step):
            if gather:
                for g in range(step):
                    for m in range(fan):
                        gathered(part * step + g, m).start()
            for m in range(fan):
                tile_copy(part, m).start()
        for copy in loads:
            copy.wait()
        if keep:
            filled = pl.ds(blocks, neigh)
            hand_on = pltpu.make_async_copy(inputs.at[filled], kept.at[filled], keep_sem)
            hand_on.start()

        def compute(block):
            panel = []
            for m in range(fan):
                panel.append(inputs[block * fan + m if gather else code_of(block, m)])
            summed = jnp.dot(
                jnp.concatenate(panel, axis=1),
                jnp.concatenate([weights[m, block] for m in range(fan)], axis=0),
                preferred_element_type=jnp.float32,
            )
            place = pl.multiple_of((first + block) * width, width)
            summed = jnp.maximum(summed + bias[layer : layer + 1, pl.ds(place, width)], 0.0).astype(result.dtype)
            if final:
                outputs[:, pl.ds(pl.multiple_of(block * width, width), width)] = summed
            else:
                outputs[block] = summed

        def work(part, _):
            for sub in range(group // step):
                for m in range(fan):
                    here = weights.at[m, pl.ds((part * (group // step) + sub) * step, step)]
                    sem = weight_sems.at[part * (group // step) + sub, m]
                    pltpu.make_async_copy(here, here, sem).wait()
            for g in range(group):
                block = part * group + g
                if gather:
                    for m in range(fan):
                        place = block * fan + m
                        pltpu.make_async_copy(inputs.at[place], inputs.at[place], in_sems.at[place]).wait()
                compute(block)
            out_copy(part).start()
            return _

        lax.fori_loop(0, count // group, work, None)
        for part in range(count // group):
            out_copy(part).wait()
        if keep:
            hand_on.wait()

    anywhere = pl.BlockSpec(memory_space=pl.ANY)
    operands = [codes, own, pool, *arrived, *(array for source in held for array in source), biases]
    in_specs = [anywhere] * (len(operands) - 3) + [pl.BlockSpec(memory_space=pltpu.VMEM)]
    aliases = {}
    if target is not None:
        aliases[len(operands)] = 0
        operands.append(target)
        in_specs.append(anywhere)
    shape = (rows, blocks * width) if final else (blocks + neigh, rows, width)
    out_shape = [jax.ShapeDtypeStruct(shape, pool.dtype)]
    if keep:
        aliases[2] = 1
        out_shape.append(jax.ShapeDtypeStruct(pool.shape, pool.dtype))
    number = count * fan if gather else blocks + neigh
    out = (rows, count * width) if final else (count, rows, width)
    results = pl.pallas_call(
        kernel,
        out_shape=out_shape,
        grid_spec=pltpu.PrefetchScalarGridSpec(
            num_scalar_prefetch=2,
            in_specs=in_specs,
            out_specs=[anywhere] * len(out_shape),
            scratch_shapes=[
                pltpu.VMEM((number, rows, width), pool.dtype),
                pltpu.VMEM((fan, count, width, width), tiles[0].dtype),
                pltpu.VMEM(out, pool.dtype),
                pltpu.SemaphoreType.DMA((number,)),
                pltpu.SemaphoreType.DMA((count // step, fan)),
                pltpu.SemaphoreType.DMA((count // group,)),
                pltpu.SemaphoreType.DMA,
            ],
        ),
        input_output_aliases=aliases,
        compiler_params=pltpu.CompilerParams(vmem_limit_bytes=VMEM_LIMIT),
        cost_estimate=FREE,
    )(*operands)
    return results if keep else (results[0], pool)


def body(activations, tile_weights, biases, source_codes, send_list):
    layer_count, block_count, part_rows, width = tile_weights.shape
    fan = source_codes.shape[2]
    part_count = lax.axis_size("dom")
    neighbor_offsets = (1, 2, -1, part_count // 2)
    sharers = width // part_rows
    own = (lax.axis_index("batch") // sharers).reshape(1).astype(jnp.int32)
    codes = source_codes.reshape(-1)
    far = fan // 2
    unit = block_count // 16

    if sharers > 1:
        members = range(lax.axis_size("batch") // sharers)
        groups = [[m * sharers + s for s in range(sharers)] for m in members]
        tile_weights = lax.all_gather(tile_weights, "batch", axis=2, tiled=True, axis_index_groups=groups)

    def spread(held, first):
        for bit in range(far.bit_length() - 1):
            for m in range(1 << bit):
                held[first + m + (1 << bit)] = jax.tree.map(
                    lambda array: swapped(array, (1 << bit) * sharers), held[first + m]
                )

    last = layer_count - 1
    chunks = [(layer, 0, 16, PIECES) for layer in range(last)]
    chunks += [(last, 0, 8, PIECES), (last, 8, 4, PIECES), (last, 12, 2, 2), (last, 14, 2, 1)]
    chunks = [(layer, first * unit, count * unit, math.gcd(pieces, count * unit)) for layer, first, count, pieces in chunks]

    crossed = []
    for layer in range(layer_count):
        for mine in cut(tile_weights, [chunk[:3] for chunk in chunks if chunk[0] == layer]):
            crossed.append(swapped(mine, far * sharers))

    near = [tile_weights] + [None] * (fan - 1)
    spread(near, 0)

    def tiles_of(index, *after):
        held = list(near)
        count, pieces = chunks[index][2:]
        arrived = lax.optimization_barrier((crossed[index], *after))[0]
        held[far] = [arrived[i * count // pieces : (i + 1) * count // pieces] for i in range(pieces)]
        spread(held, far)
        held[far] = [arrived]
        return held

    current = activations
    for index, (layer, first, count, _) in enumerate(chunks):
        if first == 0:
            arrived = []
            for slot, offset in enumerate(neighbor_offsets):
                start = send_list[layer, 0, slot]
                if layer == 0:
                    block = lax.dynamic_slice(current, (0, start * width), (current.shape[0], width))
                else:
                    block = lax.dynamic_index_in_dim(current, start, 0, keepdims=False)
                if slot > 1:
                    block = lax.optimization_barrier((block, arrived[slot - 2]))[0]
                arrived.append(shifted(block, "dom", offset))
            pool, target, after = current, None, arrived
        else:
            arrived, after = [], [current]
        keep = first == 0 and count < block_count
        current, pool = run_blocks(
            layer, first, count, codes, own, pool, arrived, tiles_of(index, *after), biases, target, keep, layer == last
        )
        target = current
    return current


def solution(mesh):
    in_specs = (
        P("batch", "dom"),
        P(None, "dom", "batch", None),
        P(None, "dom"),
        P(None, "dom", None),
        P(None, "dom", None),
    )
    out_specs = P("batch", "dom")
    return jax.shard_map(body, mesh=mesh, in_specs=in_specs, out_specs=out_specs, check_vma=False)
```

```python
import math

import jax
import jax.numpy as jnp
from jax import lax
from jax.experimental import pallas as pl
from jax.experimental.pallas import tpu as pltpu
from jax.sharding import PartitionSpec as P


BOUNDARY = 3
VMEM_LIMIT = 52 * 2**20
FREE = pl.CostEstimate(flops=0, bytes_accessed=0, transcendentals=0)


def shifted(block, axis, distance):
    devices = range(lax.axis_size(axis))
    route = [((i - distance) % len(devices), i) for i in devices]
    return lax.ppermute(block, axis, route)


def swapped(block, mask):
    route = [(i, i ^ mask) for i in range(lax.axis_size("batch"))]
    return lax.ppermute(block, "batch", route)


def cut(tile_weights, chunks):
    height, width = tile_weights.shape[2:]
    moves = []
    for place, (layer, first, count) in enumerate(chunks):
        step = math.gcd(8, count)
        moves += [(place, layer, first, start, step) for start in range(0, count, step)]

    def kernel(tiles, *refs):
        targets, (room, arrive, leave) = refs[: len(chunks)], refs[len(chunks) :]
        inward, outward = [], []
        for index, (place, layer, first, start, step) in enumerate(moves):
            here = room.at[index, pl.ds(0, step)]
            source = tiles.at[layer, pl.ds(first + start, step)]
            inward.append(pltpu.make_async_copy(source, here, arrive.at[index]))
            outward.append(pltpu.make_async_copy(here, targets[place].at[pl.ds(start, step)], leave.at[index]))
        for copy in inward:
            copy.start()
        for before, after in zip(inward, outward):
            before.wait()
            after.start()
        for copy in outward:
            copy.wait()

    anywhere = pl.BlockSpec(memory_space=pl.ANY)
    return pl.pallas_call(
        kernel,
        out_shape=[jax.ShapeDtypeStruct((count, height, width), tile_weights.dtype) for _, _, count in chunks],
        in_specs=[anywhere],
        out_specs=[anywhere] * len(chunks),
        scratch_shapes=[
            pltpu.VMEM((len(moves), 8, height, width), tile_weights.dtype),
            pltpu.SemaphoreType.DMA((len(moves),)),
            pltpu.SemaphoreType.DMA((len(moves),)),
        ],
        compiler_params=pltpu.CompilerParams(vmem_limit_bytes=VMEM_LIMIT),
        cost_estimate=FREE,
    )(tile_weights)


def run_blocks(layer, first, count, codes, pool, arrived, tiles, biases, target, final):
    fan, neigh, width = len(tiles), len(arrived), arrived[0].shape[1]
    rows, blocks = pool.shape[-2], biases.shape[1] // width
    columns = pool.ndim == 2
    group = math.gcd(8, count)
    held = [source if isinstance(source, list) else [source] for source in tiles]
    step = group
    for source in held:
        for array in source:
            step = math.gcd(step, array.shape[-3])
    parts = count // step

    def kernel(*refs):
        refs = list(refs)
        codes, pool_ref = (refs.pop(0) for _ in range(2))
        arrived_refs = [refs.pop(0) for _ in arrived]
        tile_refs = [[refs.pop(0) for _ in source] for source in held]
        bias = refs.pop(0)
        if target is not None:
            refs.pop(0)
        result, inputs, weights, outputs, in_sems, weight_sems, out_sems = refs

        def tile_copy(part, m):
            start = part * step
            if held[m][0].ndim == 4:
                piece = tile_refs[m][0].at[layer, pl.ds(first + start, step)]
            else:
                place, inside = 0, start
                while inside >= held[m][place].shape[0]:
                    inside -= held[m][place].shape[0]
                    place += 1
                piece = tile_refs[m][place].at[pl.ds(inside, step)]
            return pltpu.make_async_copy(piece, weights.at[m, pl.ds(start, step)], weight_sems.at[part, m])

        def out_copy(part):
            start = part * group
            if final:
                here = outputs.at[:, pl.ds(start * width, group * width)]
                there = result.at[:, pl.ds((first + start) * width, group * width)]
            else:
                here = outputs.at[pl.ds(start, group)]
                there = result.at[pl.ds(first + start, group)]
            return pltpu.make_async_copy(here, there, out_sems.at[part])

        loads = []
        for slot, source in enumerate(arrived_refs):
            loads.append((source, inputs.at[blocks + slot]))
        if columns:
            for block in range(blocks):
                loads.append((pool_ref.at[:, pl.ds(block * width, width)], inputs.at[block]))
        else:
            share = blocks // 4
            for start in range(0, blocks, share):
                loads.append((pool_ref.at[pl.ds(start, share)], inputs.at[pl.ds(start, share)]))
        loads = [pltpu.make_async_copy(*load, in_sems.at[place]) for place, load in enumerate(loads)]
        for copy in loads:
            copy.start()
        early = min(parts, max(1, 8 // step))
        for part in range(early):
            for m in range(fan):
                tile_copy(part, m).start()
        for copy in loads:
            copy.wait()
        for part in range(early, parts):
            for m in range(fan):
                tile_copy(part, m).start()

        def work(part, _):
            for sub in range(group // step):
                for m in range(fan):
                    here = weights.at[m, pl.ds((part * (group // step) + sub) * step, step)]
                    sem = weight_sems.at[part * (group // step) + sub, m]
                    pltpu.make_async_copy(here, here, sem).wait()
            for g in range(group):
                block = part * group + g
                base = (layer * blocks + first + block) * fan
                summed = jnp.dot(
                    jnp.concatenate([inputs[codes[base + m]] for m in range(fan)], axis=1),
                    jnp.concatenate([weights[m, block] for m in range(fan)], axis=0),
                    preferred_element_type=jnp.float32,
                )
                place = pl.multiple_of((first + block) * width, width)
                summed = summed + bias[layer : layer + 1, pl.ds(place, width)]
                summed = jnp.maximum(summed, 0.0).astype(result.dtype)
                if final:
                    outputs[:, pl.ds(pl.multiple_of(block * width, width), width)] = summed
                else:
                    outputs[block] = summed
            out_copy(part).start()
            return _

        lax.fori_loop(0, count // group, work, None)
        for part in range(count // group):
            out_copy(part).wait()

    anywhere = pl.BlockSpec(memory_space=pl.ANY)
    operands = [codes, pool, *arrived, *(array for source in held for array in source), biases]
    in_specs = [anywhere] * (len(operands) - 2) + [pl.BlockSpec(memory_space=pltpu.VMEM)]
    aliases = {}
    if target is not None:
        aliases[len(operands)] = 0
        operands.append(target)
        in_specs.append(anywhere)
    shape = (rows, blocks * width) if final else (blocks, rows, width)
    out = (rows, count * width) if final else (count, rows, width)
    return pl.pallas_call(
        kernel,
        out_shape=jax.ShapeDtypeStruct(shape, pool.dtype),
        grid_spec=pltpu.PrefetchScalarGridSpec(
            num_scalar_prefetch=1,
            in_specs=in_specs,
            out_specs=anywhere,
            scratch_shapes=[
                pltpu.VMEM((blocks + neigh, rows, width), pool.dtype),
                pltpu.VMEM((fan, count, width, width), tiles[0].dtype),
                pltpu.VMEM(out, pool.dtype),
                pltpu.SemaphoreType.DMA((blocks + neigh,)),
                pltpu.SemaphoreType.DMA((parts, fan)),
                pltpu.SemaphoreType.DMA((count // group,)),
            ],
        ),
        input_output_aliases=aliases,
        compiler_params=pltpu.CompilerParams(vmem_limit_bytes=VMEM_LIMIT),
        cost_estimate=FREE,
    )(*operands)


def body(activations, tile_weights, biases, source_codes, send_list):
    layer_count, block_count, part_rows, width = tile_weights.shape
    fan = source_codes.shape[2]
    part_count = lax.axis_size("dom")
    neighbor_offsets = (1, 2, -1, part_count // 2)
    sharers = width // part_rows
    own = lax.axis_index("batch") // sharers
    codes = jnp.take(source_codes, own ^ jnp.arange(fan), axis=2).reshape(-1)
    far = fan // 2
    unit = block_count // 16

    if sharers > 1:
        members = range(lax.axis_size("batch") // sharers)
        groups = [[m * sharers + s for s in range(sharers)] for m in members]
        tile_weights = lax.all_gather(tile_weights, "batch", axis=2, tiled=True, axis_index_groups=groups)

    def spread(held, first):
        for bit in range(far.bit_length() - 1):
            for m in range(1 << bit):
                held[first + m + (1 << bit)] = jax.tree.map(
                    lambda array: swapped(array, (1 << bit) * sharers), held[first + m]
                )

    last = layer_count - 1
    shares = [(layer, (16,), (4,)) for layer in range(last - 1)]
    shares += [(last - 1, (12, 4), (3, 1))]
    shares += [(last, (8, 4), (2, 2)), (last, (4,), (1,))]

    moves = {layer: [] for layer in range(layer_count)}
    for layer, sizes, _ in shares:
        for size in sizes:
            start = sum(count for _, _, count in moves[layer])
            moves[layer].append((layer, start, size * unit))
    crossed = {}
    for layer in moves:
        crossed[layer] = [swapped(mine, far * sharers) for mine in cut(tile_weights, moves[layer])]

    near = [tile_weights] + [None] * (fan - 1)
    spread(near, 0)

    current = activations
    before = None
    for layer, sizes, pieces in shares:
        if layer != before:
            arrived = []
            for slot, offset in enumerate(neighbor_offsets):
                start = send_list[layer, 0, slot]
                if layer == 0:
                    block = lax.dynamic_slice(current, (0, start * width), (current.shape[0], width))
                else:
                    block = lax.dynamic_index_in_dim(current, start, 0, keepdims=False)
                if slot >= BOUNDARY:
                    block = lax.optimization_barrier((block, arrived[slot - BOUNDARY]))[0]
                arrived.append(shifted(block, "dom", offset))
            pool, target, first, after = current, None, 0, arrived
        before = layer
        tiles = list(near)
        tiles[far], passed = [], []
        for number in pieces:
            tile = lax.optimization_barrier((crossed[layer].pop(0), *after))[0]
            share = tile.shape[0] // math.gcd(number, tile.shape[0])
            tiles[far].append(tile)
            passed += [tile[start : start + share] for start in range(0, tile.shape[0], share)]
        whole, tiles[far] = tiles[far], passed
        spread(tiles, far)
        tiles[far] = whole
        count = sum(sizes) * unit
        target = run_blocks(layer, first, count, codes, pool, arrived, tiles, biases, target, layer == last)
        current, first, after = target, first + count, [target]
    return current


def solution(mesh):
    in_specs = (
        P("batch", "dom"),
        P(None, "dom", "batch", None),
        P(None, "dom"),
        P(None, "dom", None),
        P(None, "dom", None),
    )
    out_specs = P("batch", "dom")
    return jax.shard_map(body, mesh=mesh, in_specs=in_specs, out_specs=out_specs, check_vma=False)
```

```python
import math

import jax
import jax.numpy as jnp
from jax import lax
from jax.experimental import pallas as pl
from jax.experimental.pallas import tpu as pltpu
from jax.sharding import PartitionSpec as P


TURNS = (3, 1, 0, 2)
VMEM_LIMIT = 52 * 2**20
LAYER_LIMIT = 48 * 2**20
FREE = pl.CostEstimate(flops=0, bytes_accessed=0, transcendentals=0)


def shifted(block, axis, distance):
    devices = range(lax.axis_size(axis))
    route = [((i - distance) % len(devices), i) for i in devices]
    return lax.ppermute(block, axis, route)


def swapped(block, mask):
    route = [(i, i ^ mask) for i in range(lax.axis_size("batch"))]
    return lax.ppermute(block, "batch", route)


def cut(tile_weights, chunks):
    height, width = tile_weights.shape[2:]
    moves = []
    for place, (layer, first, count) in enumerate(chunks):
        step = math.gcd(8, count)
        moves += [(place, layer, first, start, step) for start in range(0, count, step)]

    def kernel(tiles, *refs):
        targets, (room, arrive, leave) = refs[: len(chunks)], refs[len(chunks) :]
        inward, outward = [], []
        for index, (place, layer, first, start, step) in enumerate(moves):
            here = room.at[index, pl.ds(0, step)]
            source = tiles.at[layer, pl.ds(first + start, step)]
            inward.append(pltpu.make_async_copy(source, here, arrive.at[index]))
            outward.append(pltpu.make_async_copy(here, targets[place].at[pl.ds(start, step)], leave.at[index]))
        for copy in inward:
            copy.start()
        for before, after in zip(inward, outward):
            before.wait()
            after.start()
        for copy in outward:
            copy.wait()

    anywhere = pl.BlockSpec(memory_space=pl.ANY)
    return pl.pallas_call(
        kernel,
        out_shape=[jax.ShapeDtypeStruct((count, height, width), tile_weights.dtype) for _, _, count in chunks],
        in_specs=[anywhere],
        out_specs=[anywhere] * len(chunks),
        scratch_shapes=[
            pltpu.VMEM((len(moves), 8, height, width), tile_weights.dtype),
            pltpu.SemaphoreType.DMA((len(moves),)),
            pltpu.SemaphoreType.DMA((len(moves),)),
        ],
        compiler_params=pltpu.CompilerParams(vmem_limit_bytes=VMEM_LIMIT),
        cost_estimate=FREE,
    )(tile_weights)


def pick(table, place, number, width, activations):
    rows = activations.shape[0]

    def kernel(table, source, *refs):
        targets, semaphores = refs[:number], refs[number]
        copies = []
        for slot in range(number):
            start = pl.multiple_of(table[place + slot] * width, width)
            copies.append(pltpu.make_async_copy(source.at[:, pl.ds(start, width)], targets[slot], semaphores.at[slot]))
        for copy in copies:
            copy.start()
        for copy in copies:
            copy.wait()

    return pl.pallas_call(
        kernel,
        out_shape=[jax.ShapeDtypeStruct((rows, width), activations.dtype)] * number,
        grid_spec=pltpu.PrefetchScalarGridSpec(
            num_scalar_prefetch=1,
            in_specs=[pl.BlockSpec(memory_space=pl.ANY)],
            out_specs=[pl.BlockSpec(memory_space=pltpu.VMEM)] * number,
            scratch_shapes=[pltpu.SemaphoreType.DMA((number,))],
        ),
        compiler_params=pltpu.CompilerParams(vmem_limit_bytes=VMEM_LIMIT),
        cost_estimate=FREE,
    )(table, activations)


def run_blocks(layer, first, count, table, sends, pool, arrived, tiles, biases, target, final):
    fan, neigh, width = len(tiles), len(arrived), arrived[0].shape[1]
    rows, blocks = pool.shape[-2], biases.shape[1] // width
    columns = pool.ndim == 2
    group = math.gcd(8, count)
    held = [source if isinstance(source, list) else [source] for source in tiles]
    step = group
    for source in held:
        for array in source:
            step = math.gcd(step, array.shape[-3])
    parts = count // step

    def kernel(*refs):
        refs = list(refs)
        table, pool_ref = (refs.pop(0) for _ in range(2))
        arrived_refs = [refs.pop(0) for _ in arrived]
        tile_refs = [[refs.pop(0) for _ in source] for source in held]
        bias = refs.pop(0)
        if target is not None:
            refs.pop(0)
        result = refs.pop(0)
        outgoing = [] if final else [refs.pop(0) for _ in arrived]
        inputs, weights, outputs, in_sems, weight_sems, out_sems, send_sems = refs

        def tile_copy(part, m):
            start = part * step
            if held[m][0].ndim == 4:
                piece = tile_refs[m][0].at[layer, pl.ds(first + start, step)]
            else:
                place, inside = 0, start
                while inside >= held[m][place].shape[0]:
                    inside -= held[m][place].shape[0]
                    place += 1
                piece = tile_refs[m][place].at[pl.ds(inside, step)]
            return pltpu.make_async_copy(piece, weights.at[m, pl.ds(start, step)], weight_sems.at[part, m])

        def out_copy(part):
            start = part * group
            if final:
                here = outputs.at[:, pl.ds(start * width, group * width)]
                there = result.at[:, pl.ds((first + start) * width, group * width)]
            else:
                here = outputs.at[pl.ds(start, group)]
                there = result.at[pl.ds(first + start, group)]
            return pltpu.make_async_copy(here, there, out_sems.at[part])

        loads = []
        for slot, source in enumerate(arrived_refs):
            loads.append((source, inputs.at[blocks + slot]))
        if columns:
            for block in range(blocks):
                loads.append((pool_ref.at[:, pl.ds(block * width, width)], inputs.at[block]))
        else:
            share = blocks // 4
            for start in range(0, blocks, share):
                loads.append((pool_ref.at[pl.ds(start, share)], inputs.at[pl.ds(start, share)]))
        loads = [pltpu.make_async_copy(*load, in_sems.at[place]) for place, load in enumerate(loads)]
        for copy in loads:
            copy.start()
        early = min(parts, max(1, 8 // step))
        for part in range(early):
            for m in range(fan):
                tile_copy(part, m).start()
        for copy in loads:
            copy.wait()
        for part in range(early, parts):
            for m in range(fan):
                tile_copy(part, m).start()

        def work(part, _):
            for sub in range(group // step):
                for m in range(fan):
                    here = weights.at[m, pl.ds((part * (group // step) + sub) * step, step)]
                    sem = weight_sems.at[part * (group // step) + sub, m]
                    pltpu.make_async_copy(here, here, sem).wait()
            for g in range(group):
                block = part * group + g
                base = (layer * blocks + first + block) * fan
                summed = jnp.dot(
                    jnp.concatenate([inputs[table[base + m]] for m in range(fan)], axis=1),
                    jnp.concatenate([weights[m, block] for m in range(fan)], axis=0),
                    preferred_element_type=jnp.float32,
                )
                place = pl.multiple_of((first + block) * width, width)
                summed = summed + bias[layer : layer + 1, pl.ds(place, width)]
                summed = jnp.maximum(summed, 0.0).astype(result.dtype)
                if final:
                    outputs[:, pl.ds(pl.multiple_of(block * width, width), width)] = summed
                else:
                    outputs[block] = summed
            out_copy(part).start()
            return _

        lax.fori_loop(0, count // group, work, None)
        handed = []
        for slot, there in enumerate(outgoing):
            handed.append(pltpu.make_async_copy(outputs.at[table[sends + slot]], there, send_sems.at[slot]))
            handed[-1].start()
        for copy in handed:
            copy.wait()
        for part in range(count // group):
            out_copy(part).wait()

    anywhere = pl.BlockSpec(memory_space=pl.ANY)
    operands = [table, pool, *arrived, *(array for source in held for array in source), biases]
    in_specs = [anywhere] * (len(operands) - 2) + [pl.BlockSpec(memory_space=pltpu.VMEM)]
    aliases = {}
    if target is not None:
        aliases[len(operands)] = 0
        operands.append(target)
        in_specs.append(anywhere)
    shape = (rows, blocks * width) if final else (blocks, rows, width)
    out = (rows, count * width) if final else (count, rows, width)
    out_shape = [jax.ShapeDtypeStruct(shape, pool.dtype)]
    if not final:
        out_shape += [jax.ShapeDtypeStruct((rows, width), pool.dtype)] * neigh
    result, *outgoing = pl.pallas_call(
        kernel,
        out_shape=out_shape,
        grid_spec=pltpu.PrefetchScalarGridSpec(
            num_scalar_prefetch=1,
            in_specs=in_specs,
            out_specs=[anywhere] * len(out_shape),
            scratch_shapes=[
                pltpu.VMEM((blocks + neigh, rows, width), pool.dtype),
                pltpu.VMEM((fan, count, width, width), tiles[0].dtype),
                pltpu.VMEM(out, pool.dtype),
                pltpu.SemaphoreType.DMA((blocks + neigh,)),
                pltpu.SemaphoreType.DMA((parts, fan)),
                pltpu.SemaphoreType.DMA((count // group,)),
                pltpu.SemaphoreType.DMA((neigh,)),
            ],
        ),
        input_output_aliases=aliases,
        compiler_params=pltpu.CompilerParams(vmem_limit_bytes=LAYER_LIMIT),
        cost_estimate=FREE,
    )(*operands)
    return result, outgoing


def body(activations, tile_weights, biases, source_codes, send_list):
    layer_count, block_count, part_rows, width = tile_weights.shape
    fan = source_codes.shape[2]
    part_count = lax.axis_size("dom")
    neighbor_offsets = (1, 2, -1, part_count // 2)
    sharers = width // part_rows
    own = lax.axis_index("batch") // sharers
    codes = jnp.take(source_codes, own ^ jnp.arange(fan), axis=2).reshape(-1)
    table = jnp.concatenate([codes, send_list.reshape(-1)])
    far = fan // 2
    unit = block_count // 16

    if sharers > 1:
        members = range(lax.axis_size("batch") // sharers)
        groups = [[m * sharers + s for s in range(sharers)] for m in members]
        tile_weights = lax.all_gather(tile_weights, "batch", axis=2, tiled=True, axis_index_groups=groups)

    def spread(held, first):
        for bit in range(far.bit_length() - 1):
            for m in range(1 << bit):
                held[first + m + (1 << bit)] = jax.tree.map(
                    lambda array: swapped(array, (1 << bit) * sharers), held[first + m]
                )

    last = layer_count - 1
    shares = [(layer, (16,), (4,)) for layer in range(last - 1)]
    shares += [(last - 1, (12, 4), (3, 1))]
    shares += [(last, (8, 4), (2, 2)), (last, (4,), (1,))]

    moves = {layer: [] for layer in range(layer_count)}
    for layer, sizes, _ in shares:
        for size in sizes:
            start = sum(count for _, _, count in moves[layer])
            moves[layer].append((layer, start, size * unit))
    crossed = {}
    for layer in moves:
        crossed[layer] = [swapped(mine, far * sharers) for mine in cut(tile_weights, moves[layer])]

    near = [tile_weights] + [None] * (fan - 1)
    spread(near, 0)

    current = activations
    neigh = len(neighbor_offsets)
    outgoing = pick(table, codes.size, neigh, width, activations)
    before = None
    for layer, sizes, pieces in shares:
        if layer != before:
            arrived = [None] * neigh
            for turn, slot in enumerate(TURNS):
                block = outgoing[slot]
                if turn == neigh - 1:
                    block = lax.optimization_barrier((block, arrived[TURNS[1]]))[0]
                arrived[slot] = shifted(block, "dom", neighbor_offsets[slot])
            pool, target, first, after = current, None, 0, arrived
        before = layer
        tiles = list(near)
        tiles[far], passed = [], []
        for number in pieces:
            tile = lax.optimization_barrier((crossed[layer].pop(0), *after))[0]
            share = tile.shape[0] // math.gcd(number, tile.shape[0])
            tiles[far].append(tile)
            passed += [tile[start : start + share] for start in range(0, tile.shape[0], share)]
        whole, tiles[far] = tiles[far], passed
        spread(tiles, far)
        tiles[far] = whole
        count = sum(sizes) * unit
        sends = codes.size + (layer + 1) * neigh
        target, outgoing = run_blocks(
            layer, first, count, table, sends, pool, arrived, tiles, biases, target, layer == last
        )
        current, first, after = target, first + count, [target]
    return current


def solution(mesh):
    in_specs = (
        P("batch", "dom"),
        P(None, "dom", "batch", None),
        P(None, "dom"),
        P(None, "dom", None),
        P(None, "dom", None),
    )
    out_specs = P("batch", "dom")
    return jax.shard_map(body, mesh=mesh, in_specs=in_specs, out_specs=out_specs, check_vma=False)
```

```python
import math

import jax
import jax.numpy as jnp
from jax import lax
from jax.experimental import pallas as pl
from jax.experimental.pallas import tpu as pltpu
from jax.sharding import PartitionSpec as P


TURNS = (3, 1, 0, 2)
NEIGH = 4
VMEM_LIMIT = 16 * 2**20
LAYER_LIMIT = 20 * 2**20
FREE = pl.CostEstimate(flops=0, bytes_accessed=0, transcendentals=0)


def shifted(block, axis, distance):
    devices = range(lax.axis_size(axis))
    route = [((i - distance) % len(devices), i) for i in devices]
    return lax.ppermute(block, axis, route)


def swapped(block, mask):
    route = [(i, i ^ mask) for i in range(lax.axis_size("batch"))]
    return lax.ppermute(block, "batch", route)


def in_hbm(array):
    return pltpu.with_memory_space_constraint(array, pltpu.HBM)


def in_vmem(array):
    return pltpu.with_memory_space_constraint(array, pltpu.VMEM)


def cut(tile_weights, chunks):
    height, width = tile_weights.shape[2:]

    def kernel(tiles, *refs):
        targets, semaphores = refs[: len(chunks)], refs[len(chunks)]
        copies = []
        for place, (layer, first, count) in enumerate(chunks):
            step = count // math.gcd(4, count)
            for part, start in enumerate(range(0, count, step)):
                source = tiles.at[layer, pl.ds(first + start, step)]
                there = targets[place].at[pl.ds(start, step)]
                copies.append(pltpu.make_async_copy(source, there, semaphores.at[place, part]))
        for copy in copies:
            copy.start()
        for copy in copies:
            copy.wait()

    return pl.pallas_call(
        kernel,
        out_shape=[pltpu.VMEM((count, height, width), tile_weights.dtype) for _, _, count in chunks],
        in_specs=[pl.BlockSpec(memory_space=pltpu.HBM)],
        out_specs=[pl.BlockSpec(memory_space=pltpu.VMEM)] * len(chunks),
        scratch_shapes=[pltpu.SemaphoreType.DMA((len(chunks), 4))],
        compiler_params=pltpu.CompilerParams(vmem_limit_bytes=VMEM_LIMIT),
        cost_estimate=FREE,
    )(in_hbm(tile_weights))


def pick(table, place, number, width, activations):
    rows = activations.shape[0]

    def kernel(table, source, *refs):
        targets, semaphores = refs[:number], refs[number]
        copies = []
        for slot in range(number):
            start = pl.multiple_of(table[place + slot] * width, width)
            copies.append(pltpu.make_async_copy(source.at[:, pl.ds(start, width)], targets[slot], semaphores.at[slot]))
        for copy in copies:
            copy.start()
        for copy in copies:
            copy.wait()

    return pl.pallas_call(
        kernel,
        out_shape=[jax.ShapeDtypeStruct((rows, width), activations.dtype)] * number,
        grid_spec=pltpu.PrefetchScalarGridSpec(
            num_scalar_prefetch=1,
            in_specs=[pl.BlockSpec(memory_space=pltpu.HBM)],
            out_specs=[pl.BlockSpec(memory_space=pltpu.VMEM)] * number,
            scratch_shapes=[pltpu.SemaphoreType.DMA((number,))],
        ),
        compiler_params=pltpu.CompilerParams(vmem_limit_bytes=VMEM_LIMIT),
        cost_estimate=FREE,
    )(table, in_hbm(activations))


def run_blocks(layer, first, count, table, sends, pool, arrived, tiles, biases, target, final):
    fan, width = len(tiles), tiles[0].shape[3]
    rows, blocks = pool.shape[-2], biases.shape[1] // width
    columns = pool.ndim == 2
    fill = bool(arrived) and not columns
    group = math.gcd(8, count)
    held = [source if isinstance(source, list) else [source] for source in tiles]
    step = group
    for source in held:
        for array in source:
            step = math.gcd(step, array.shape[-3])
    parts = count // step

    def kernel(*refs):
        refs = list(refs)
        table, pool_ref = (refs.pop(0) for _ in range(2))
        arrived_refs = [refs.pop(0) for _ in arrived]
        tile_refs = [[refs.pop(0) for _ in source] for source in held]
        bias = refs.pop(0)
        if target is not None:
            refs.pop(0)
        result = refs.pop(0)
        inputs = refs.pop(0) if fill else pool_ref
        outgoing = [] if final else [refs.pop(0) for _ in range(neigh)]
        weights, in_sems, weight_sems = (refs.pop(0) for _ in range(3))
        if final:
            outputs, out_sems = (refs.pop(0) for _ in range(2))
        if columns:
            inputs = refs.pop(0)

        def tile_copy(part, m):
            start = part * step
            if held[m][0].ndim == 4:
                piece = tile_refs[m][0].at[layer, pl.ds(first + start, step)]
            else:
                place, inside = 0, start
                while inside >= held[m][place].shape[0]:
                    inside -= held[m][place].shape[0]
                    place += 1
                piece = tile_refs[m][place].at[pl.ds(inside, step)]
            return pltpu.make_async_copy(piece, weights.at[m, pl.ds(start, step)], weight_sems.at[part, m])

        def out_copy(part):
            here = outputs.at[:, pl.ds(part * group * width, group * width)]
            there = result.at[:, pl.ds((first + part * group) * width, group * width)]
            return pltpu.make_async_copy(here, there, out_sems.at[part])

        loads = []
        for slot, source in enumerate(arrived_refs):
            loads.append((source, inputs.at[blocks + slot]))
        if columns:
            for block in range(blocks):
                loads.append((pool_ref.at[:, pl.ds(block * width, width)], inputs.at[block]))
        loads = [pltpu.make_async_copy(*load, in_sems.at[place]) for place, load in enumerate(loads)]
        for copy in loads:
            copy.start()
        for part in range(parts):
            for m in range(fan):
                tile_copy(part, m).start()
        for copy in loads:
            copy.wait()

        def work(part, _):
            for sub in range(group // step):
                for m in range(fan):
                    here = weights.at[m, pl.ds((part * (group // step) + sub) * step, step)]
                    sem = weight_sems.at[part * (group // step) + sub, m]
                    pltpu.make_async_copy(here, here, sem).wait()
            for g in range(group):
                block = part * group + g
                base = (layer * blocks + first + block) * fan
                summed = jnp.dot(
                    jnp.concatenate([inputs[table[base + m]] for m in range(fan)], axis=1),
                    jnp.concatenate([weights[m, block] for m in range(fan)], axis=0),
                    preferred_element_type=jnp.float32,
                )
                place = pl.multiple_of((first + block) * width, width)
                summed = summed + bias[layer : layer + 1, pl.ds(place, width)]
                summed = jnp.maximum(summed, 0.0).astype(result.dtype)
                if final:
                    outputs[:, pl.ds(pl.multiple_of(block * width, width), width)] = summed
                else:
                    result[first + block] = summed
            if final:
                out_copy(part).start()
            return _

        lax.fori_loop(0, count // group, work, None)
        for slot, there in enumerate(outgoing):
            there[...] = result[table[sends + slot]]
        if final:
            for part in range(count // group):
                out_copy(part).wait()

    anywhere = pl.BlockSpec(memory_space=pl.ANY)
    vmem, hbm = (pl.BlockSpec(memory_space=space) for space in (pltpu.VMEM, pltpu.HBM))
    neigh = NEIGH
    operands = [table, in_hbm(pool) if columns else in_vmem(pool), *arrived]
    in_specs = [hbm if columns else vmem] + [anywhere] * len(arrived)
    for source in tiles:
        if isinstance(source, list):
            operands += source
            in_specs += [anywhere] * len(source)
        else:
            operands.append(in_hbm(source))
            in_specs.append(hbm)
    operands.append(biases)
    in_specs.append(vmem)
    aliases = {}
    if target is not None:
        aliases[len(operands)] = 0
        operands.append(target)
        in_specs.append(anywhere)
    if final:
        out_shape, out_specs = [jax.ShapeDtypeStruct((rows, blocks * width), pool.dtype)], [anywhere]
    else:
        out_shape, out_specs = [pltpu.VMEM((blocks + neigh, rows, width), pool.dtype)], [vmem]
    if fill:
        aliases[1] = 1
        out_shape.append(pltpu.VMEM(pool.shape, pool.dtype))
        out_specs.append(vmem)
    if not final:
        out_shape += [jax.ShapeDtypeStruct((rows, width), pool.dtype)] * neigh
        out_specs += [vmem] * neigh
    scratch = [
        pltpu.VMEM((fan, count, width, width), tiles[0].dtype),
        pltpu.SemaphoreType.DMA((blocks + neigh,)),
        pltpu.SemaphoreType.DMA((parts, fan)),
    ]
    if final:
        scratch += [pltpu.VMEM((rows, count * width), pool.dtype), pltpu.SemaphoreType.DMA((count // group,))]
    if columns:
        scratch.append(pltpu.VMEM((blocks + neigh, rows, width), pool.dtype))
    results = list(
        pl.pallas_call(
            kernel,
            out_shape=out_shape,
            grid_spec=pltpu.PrefetchScalarGridSpec(
                num_scalar_prefetch=1, in_specs=in_specs, out_specs=out_specs, scratch_shapes=scratch
            ),
            input_output_aliases=aliases,
            compiler_params=pltpu.CompilerParams(vmem_limit_bytes=LAYER_LIMIT),
            cost_estimate=FREE,
        )(*operands)
    )
    return results.pop(0), results.pop(0) if fill else pool, results


def body(activations, tile_weights, biases, source_codes, send_list):
    layer_count, block_count, part_rows, width = tile_weights.shape
    fan = source_codes.shape[2]
    part_count = lax.axis_size("dom")
    neighbor_offsets = (1, 2, -1, part_count // 2)
    sharers = width // part_rows
    own = lax.axis_index("batch") // sharers
    codes = jnp.take(source_codes, own ^ jnp.arange(fan), axis=2).reshape(-1)
    table = jnp.concatenate([codes, send_list.reshape(-1)])
    far = fan // 2
    unit = block_count // 16

    if sharers > 1:
        members = range(lax.axis_size("batch") // sharers)
        groups = [[m * sharers + s for s in range(sharers)] for m in members]
        tile_weights = lax.all_gather(tile_weights, "batch", axis=2, tiled=True, axis_index_groups=groups)

    def spread(held, first):
        for bit in range(far.bit_length() - 1):
            for m in range(1 << bit):
                held[first + m + (1 << bit)] = jax.tree.map(
                    lambda array: swapped(array, (1 << bit) * sharers), held[first + m]
                )

    last = layer_count - 1
    shares = [(layer, (16,), (4,)) for layer in range(last - 1)]
    shares += [(last - 1, (12, 4), (3, 1))]
    shares += [(last, (8, 4), (2, 2)), (last, (4,), (1,))]

    moves = {layer: [] for layer in range(layer_count)}
    for layer, sizes, _ in shares:
        for size in sizes:
            start = sum(count for _, _, count in moves[layer])
            moves[layer].append((layer, start, size * unit))
    crossed = {}
    for layer in moves:
        crossed[layer] = [swapped(mine, far * sharers) for mine in cut(tile_weights, moves[layer])]

    near = [tile_weights] + [None] * (fan - 1)
    spread(near, 0)

    current = activations
    outgoing = pick(table, codes.size, NEIGH, width, activations)
    before = None
    for layer, sizes, pieces in shares:
        if layer != before:
            arrived = [None] * NEIGH
            for turn, slot in enumerate(TURNS):
                block = outgoing[slot]
                if turn == NEIGH - 1:
                    block = lax.optimization_barrier((block, arrived[TURNS[1]]))[0]
                arrived[slot] = shifted(block, "dom", neighbor_offsets[slot])
            pool, target, first, after = current, None, 0, arrived
        before = layer
        tiles = list(near)
        tiles[far], passed = [], []
        for number in pieces:
            tile = lax.optimization_barrier((crossed[layer].pop(0), *after))[0]
            share = tile.shape[0] // math.gcd(number, tile.shape[0])
            tiles[far].append(tile)
            passed += [tile[start : start + share] for start in range(0, tile.shape[0], share)]
        whole, tiles[far] = tiles[far], passed
        spread(tiles, far)
        tiles[far] = whole
        count = sum(sizes) * unit
        sends = codes.size + (layer + 1) * NEIGH
        target, pool, outgoing = run_blocks(
            layer, first, count, table, sends, pool, arrived, tiles, biases, target, layer == last
        )
        arrived = []
        current, first, after = target, first + count, [target]
    return current


def solution(mesh):
    in_specs = (
        P("batch", "dom"),
        P(None, "dom", "batch", None),
        P(None, "dom"),
        P(None, "dom", None),
        P(None, "dom", None),
    )
    out_specs = P("batch", "dom")
    return jax.shard_map(body, mesh=mesh, in_specs=in_specs, out_specs=out_specs, check_vma=False)
```

```python
import functools
import math

import jax
import jax.numpy as jnp
from jax import lax
from jax.experimental import pallas as pl
from jax.experimental.pallas import tpu as pltpu
from jax.sharding import PartitionSpec as P

TURNS = (3, 1, 0, 2)
BOUNDARY = 2
CUTS = 16
NEIGH = 4
VMEM_LIMIT = 16 * 2**20
LAYER_LIMIT = 20 * 2**20
FREE = pl.CostEstimate(flops=0, bytes_accessed=0, transcendentals=0)


def shifted(block, axis, distance):
    devices = range(lax.axis_size(axis))
    route = [((i - distance) % len(devices), i) for i in devices]
    return lax.ppermute(block, axis, route)


def swapped(block, mask):
    route = [(i, i ^ mask) for i in range(lax.axis_size("batch"))]
    return lax.ppermute(block, "batch", route)


def in_hbm(array):
    return pltpu.with_memory_space_constraint(array, pltpu.HBM)


def in_vmem(array):
    return pltpu.with_memory_space_constraint(array, pltpu.VMEM)


def cut(tile_weights, chunks):
    height, width = tile_weights.shape[2:]

    def kernel(tiles, *refs):
        targets, semaphores = refs[: len(chunks)], refs[len(chunks)]
        copies = []
        for place, (layer, first, count) in enumerate(chunks):
            step = count // math.gcd(CUTS, count)
            for part, start in enumerate(range(0, count, step)):
                source = tiles.at[layer, pl.ds(first + start, step)]
                there = targets[place].at[pl.ds(start, step)]
                copies.append(pltpu.make_async_copy(source, there, semaphores.at[place, part]))
        for copy in copies:
            copy.start()
        for copy in copies:
            copy.wait()

    parts = pl.pallas_call(
        kernel,
        out_shape=[pltpu.VMEM((count, height, width), tile_weights.dtype) for _, _, count in chunks],
        in_specs=[pl.BlockSpec(memory_space=pltpu.HBM)],
        out_specs=[pl.BlockSpec(memory_space=pltpu.VMEM)] * len(chunks),
        scratch_shapes=[pltpu.SemaphoreType.DMA((len(chunks), CUTS))],
        compiler_params=pltpu.CompilerParams(vmem_limit_bytes=VMEM_LIMIT),
        cost_estimate=FREE,
    )(in_hbm(tile_weights))
    return list(parts)


def pick(table, place, number, width, activations):
    rows = activations.shape[0]

    def kernel(table, source, *refs):
        targets, semaphores = refs[:number], refs[number]
        copies = []
        for slot in range(number):
            start = pl.multiple_of(table[place + slot] * width, width)
            copies.append(pltpu.make_async_copy(source.at[:, pl.ds(start, width)], targets[slot], semaphores.at[slot]))
        for copy in copies:
            copy.start()
        for copy in copies:
            copy.wait()

    return pl.pallas_call(
        kernel,
        out_shape=[jax.ShapeDtypeStruct((rows, width), activations.dtype)] * number,
        grid_spec=pltpu.PrefetchScalarGridSpec(
            num_scalar_prefetch=1,
            in_specs=[pl.BlockSpec(memory_space=pltpu.HBM)],
            out_specs=[pl.BlockSpec(memory_space=pltpu.VMEM)] * number,
            scratch_shapes=[pltpu.SemaphoreType.DMA((number,))],
        ),
        compiler_params=pltpu.CompilerParams(vmem_limit_bytes=VMEM_LIMIT),
        cost_estimate=FREE,
    )(table, in_hbm(activations))


def run_blocks(layer, first, count, table, sends, pool, arrived, tiles, biases, target, final):
    fan, width = len(tiles), tiles[0][0].shape[2]
    rows, blocks = pool.shape[-2], biases.shape[1] // width
    columns = pool.ndim == 2
    fill = bool(arrived) and not columns
    places = {}
    for m in range(fan):
        places[m] = [(part, inside) for part, array in enumerate(tiles[m]) for inside in range(array.shape[0])]
    cuts = [block for block in range(count) if any(places[m][block][1] == 0 for m in range(fan))] + [count]
    group = math.gcd(8, *cuts)

    def kernel(*refs):
        refs = list(refs)
        table, pool_ref = (refs.pop(0) for _ in range(2))
        arrived_refs = [refs.pop(0) for _ in arrived]
        tile_refs = [[refs.pop(0) for _ in source] for source in tiles]
        bias = refs.pop(0)
        if target is not None:
            refs.pop(0)
        result = refs.pop(0)
        inputs = refs.pop(0) if fill else pool_ref
        outgoing = [] if final else [refs.pop(0) for _ in range(neigh)]
        in_sems = refs.pop(0)
        if final:
            outputs, out_sems = (refs.pop(0) for _ in range(2))
        if columns:
            inputs = refs.pop(0)

        def out_copy(part):
            here = outputs.at[:, pl.ds(part * group * width, group * width)]
            there = result.at[:, pl.ds((first + part * group) * width, group * width)]
            return pltpu.make_async_copy(here, there, out_sems.at[part])

        loads = []
        for slot, source in enumerate(arrived_refs):
            loads.append((source, inputs.at[blocks + slot]))
        if columns:
            for block in range(blocks):
                loads.append((pool_ref.at[:, pl.ds(block * width, width)], inputs.at[block]))
        loads = [pltpu.make_async_copy(*load, in_sems.at[place]) for place, load in enumerate(loads)]
        for copy in loads:
            copy.start()
        for copy in loads:
            copy.wait()

        def work(start, part, _):
            for g in range(group):
                block = part * group + g
                base = (layer * blocks + first + block) * fan
                weights = []
                for m in range(fan):
                    place, inside = places[m][start]
                    weights.append(tile_refs[m][place][block - start + inside])
                summed = jnp.dot(
                    jnp.concatenate([inputs[table[base + m]] for m in range(fan)], axis=1),
                    jnp.concatenate(weights, axis=0),
                    preferred_element_type=jnp.float32,
                )
                place = pl.multiple_of((first + block) * width, width)
                summed = summed + bias[layer : layer + 1, pl.ds(place, width)]
                summed = jnp.maximum(summed, 0.0).astype(result.dtype)
                if final:
                    outputs[:, pl.ds(pl.multiple_of(block * width, width), width)] = summed
                else:
                    result[first + block] = summed
            if final:
                out_copy(part).start()
            return _

        for start, end in zip(cuts, cuts[1:]):
            lax.fori_loop(start // group, end // group, functools.partial(work, start), None)
        for slot, there in enumerate(outgoing):
            there[...] = result[table[sends + slot]]
        if final:
            for part in range(count // group):
                out_copy(part).wait()

    anywhere = pl.BlockSpec(memory_space=pl.ANY)
    vmem, hbm = (pl.BlockSpec(memory_space=space) for space in (pltpu.VMEM, pltpu.HBM))
    neigh = NEIGH
    operands = [table, in_hbm(pool) if columns else in_vmem(pool), *arrived]
    in_specs = [hbm if columns else vmem] + [anywhere] * len(arrived)
    for source in tiles:
        operands += [in_vmem(array) for array in source]
        in_specs += [vmem] * len(source)
    operands.append(biases)
    in_specs.append(vmem)
    aliases = {}
    if target is not None:
        aliases[len(operands)] = 0
        operands.append(target)
        in_specs.append(anywhere)
    if final:
        out_shape, out_specs = [jax.ShapeDtypeStruct((rows, blocks * width), pool.dtype)], [anywhere]
    else:
        out_shape, out_specs = [pltpu.VMEM((blocks + neigh, rows, width), pool.dtype)], [vmem]
    if fill:
        aliases[1] = 1
        out_shape.append(pltpu.VMEM(pool.shape, pool.dtype))
        out_specs.append(vmem)
    if not final:
        out_shape += [jax.ShapeDtypeStruct((rows, width), pool.dtype)] * neigh
        out_specs += [vmem] * neigh
    scratch = [pltpu.SemaphoreType.DMA((blocks + neigh,))]
    if final:
        scratch += [pltpu.VMEM((rows, count * width), pool.dtype), pltpu.SemaphoreType.DMA((count // group,))]
    if columns:
        scratch.append(pltpu.VMEM((blocks + neigh, rows, width), pool.dtype))
    results = list(
        pl.pallas_call(
            kernel,
            out_shape=out_shape,
            grid_spec=pltpu.PrefetchScalarGridSpec(
                num_scalar_prefetch=1, in_specs=in_specs, out_specs=out_specs, scratch_shapes=scratch
            ),
            input_output_aliases=aliases,
            compiler_params=pltpu.CompilerParams(vmem_limit_bytes=LAYER_LIMIT),
            cost_estimate=FREE,
        )(*operands)
    )
    return results.pop(0), results.pop(0) if fill else pool, results


def body(activations, tile_weights, biases, source_codes, send_list):
    layer_count, block_count, part_rows, width = tile_weights.shape
    fan = source_codes.shape[2]
    part_count = lax.axis_size("dom")
    neighbor_offsets = (1, 2, -1, part_count // 2)
    sharers = width // part_rows
    own = lax.axis_index("batch") // sharers
    codes = jnp.take(source_codes, own ^ jnp.arange(fan), axis=2).reshape(-1)
    table = jnp.concatenate([codes, send_list.reshape(-1)])
    far = fan // 2
    unit = block_count // 16

    if sharers > 1:
        members = range(lax.axis_size("batch") // sharers)
        groups = [[m * sharers + s for s in range(sharers)] for m in members]
        tile_weights = lax.all_gather(tile_weights, "batch", axis=2, tiled=True, axis_index_groups=groups)

    def spread(held, first):
        for bit in range(far.bit_length() - 1):
            for m in range(1 << bit):
                held[first + m + (1 << bit)] = jax.tree.map(
                    lambda array: swapped(array, (1 << bit) * sharers), held[first + m]
                )

    last = layer_count - 1
    shares = [(layer, (16,), (4,)) for layer in range(last - 1)]
    shares += [(last - 1, (12, 4), (3, 1))]
    shares += [(last, (8, 4), (2, 2)), (last, (4,), (1,))]

    moves = {layer: [] for layer in range(layer_count)}
    for layer, sizes, _ in shares:
        for size in sizes:
            start = sum(count for _, _, count in moves[layer])
            moves[layer].append((layer, start, size * unit))
    mine = {layer: cut(tile_weights, moves[layer]) for layer in moves}
    crossed = {layer: [swapped(tile, far * sharers) for tile in mine[layer]] for layer in moves}

    whole = [tile_weights] + [None] * (fan - 1)
    spread(whole, 0)
    near = {layer: [cut(array, moves[layer]) for array in whole[1:far]] for layer in moves}

    current = activations
    outgoing = pick(table, codes.size, NEIGH, width, activations)
    before = None
    for layer, sizes, pieces in shares:
        if layer != before:
            arrived = [None] * NEIGH
            for turn, slot in enumerate(TURNS):
                block = outgoing[slot]
                if turn >= BOUNDARY:
                    block = lax.optimization_barrier((block, arrived[TURNS[turn - BOUNDARY]]))[0]
                arrived[slot] = shifted(block, "dom", neighbor_offsets[slot])
            pool, target, first, after = current, None, 0, arrived
        before = layer
        after = [*after, *(tile for source in near[layer] for tile in source)]
        tiles = [None] * fan
        for m, source in enumerate([mine[layer], *near[layer], crossed[layer]]):
            tiles[m] = [source.pop(0) for _ in sizes]
        passed = []
        for number, tile in zip(pieces, tiles[far]):
            tile = lax.optimization_barrier((tile, *after))[0]
            after = [*after, tile]
            share = tile.shape[0] // math.gcd(number, tile.shape[0])
            passed += [tile[start : start + share] for start in range(0, tile.shape[0], share)]
        held, tiles[far] = tiles[far], passed
        spread(tiles, far)
        tiles[far] = held
        count = sum(sizes) * unit
        sends = codes.size + (layer + 1) * NEIGH
        target, pool, outgoing = run_blocks(
            layer, first, count, table, sends, pool, arrived, tiles, biases, target, layer == last
        )
        arrived = []
        current, first, after = target, first + count, [target]
    return current


def solution(mesh):
    in_specs = (
        P("batch", "dom"),
        P(None, "dom", "batch", None),
        P(None, "dom"),
        P(None, "dom", None),
        P(None, "dom", None),
    )
    out_specs = P("batch", "dom")
    return jax.shard_map(body, mesh=mesh, in_specs=in_specs, out_specs=out_specs, check_vma=False)
```

```python
import functools
import math

import jax
import jax.numpy as jnp
from jax import lax
from jax.experimental import pallas as pl
from jax.experimental.pallas import tpu as pltpu
from jax.sharding import PartitionSpec as P

TURNS = (3, 1, 0, 2)
BOUNDARY = 2
CUTS = 16
NEIGH = 4
VMEM_LIMIT = 16 * 2**20
LAYER_LIMIT = 20 * 2**20
FREE = pl.CostEstimate(flops=0, bytes_accessed=0, transcendentals=0)


def shifted(block, axis, distance):
    devices = range(lax.axis_size(axis))
    route = [((i - distance) % len(devices), i) for i in devices]
    return lax.ppermute(block, axis, route)


def swapped(block, mask):
    route = [(i, i ^ mask) for i in range(lax.axis_size("batch"))]
    return lax.ppermute(block, "batch", route)


def in_hbm(array):
    return pltpu.with_memory_space_constraint(array, pltpu.HBM)


def in_vmem(array):
    return pltpu.with_memory_space_constraint(array, pltpu.VMEM)


def cut(tile_weights, chunks):
    height, width = tile_weights.shape[2:]

    def kernel(tiles, *refs):
        targets, semaphores = refs[: len(chunks)], refs[len(chunks)]
        copies = []
        for place, (layer, first, count) in enumerate(chunks):
            step = count // math.gcd(CUTS, count)
            for part, start in enumerate(range(0, count, step)):
                source = tiles.at[layer, pl.ds(first + start, step)]
                there = targets[place].at[pl.ds(start, step)]
                copies.append(pltpu.make_async_copy(source, there, semaphores.at[place, part]))
        for copy in copies:
            copy.start()
        for copy in copies:
            copy.wait()

    parts = pl.pallas_call(
        kernel,
        out_shape=[pltpu.VMEM((count, height, width), tile_weights.dtype) for _, _, count in chunks],
        in_specs=[pl.BlockSpec(memory_space=pltpu.HBM)],
        out_specs=[pl.BlockSpec(memory_space=pltpu.VMEM)] * len(chunks),
        scratch_shapes=[pltpu.SemaphoreType.DMA((len(chunks), CUTS))],
        compiler_params=pltpu.CompilerParams(vmem_limit_bytes=VMEM_LIMIT),
        cost_estimate=FREE,
    )(in_hbm(tile_weights))
    return list(parts)


def pick(table, place, number, width, activations):
    rows = activations.shape[0]

    def kernel(table, source, *refs):
        targets, semaphores = refs[:number], refs[number]
        copies = []
        for slot in range(number):
            start = pl.multiple_of(table[place + slot] * width, width)
            copies.append(pltpu.make_async_copy(source.at[:, pl.ds(start, width)], targets[slot], semaphores.at[slot]))
        for copy in copies:
            copy.start()
        for copy in copies:
            copy.wait()

    return pl.pallas_call(
        kernel,
        out_shape=[jax.ShapeDtypeStruct((rows, width), activations.dtype)] * number,
        grid_spec=pltpu.PrefetchScalarGridSpec(
            num_scalar_prefetch=1,
            in_specs=[pl.BlockSpec(memory_space=pltpu.HBM)],
            out_specs=[pl.BlockSpec(memory_space=pltpu.VMEM)] * number,
            scratch_shapes=[pltpu.SemaphoreType.DMA((number,))],
        ),
        compiler_params=pltpu.CompilerParams(vmem_limit_bytes=VMEM_LIMIT),
        cost_estimate=FREE,
    )(table, in_hbm(activations))


def run_blocks(layer, first, count, table, sends, pool, arrived, tiles, biases, target, final):
    fan, width = len(tiles), tiles[0][0].shape[2]
    rows, blocks = pool.shape[-2], biases.shape[1] // width
    columns = pool.ndim == 2
    fill = bool(arrived) and not columns
    places = {}
    for m in range(fan):
        places[m] = [(part, inside) for part, array in enumerate(tiles[m]) for inside in range(array.shape[0])]
    cuts = [block for block in range(count) if any(places[m][block][1] == 0 for m in range(fan))] + [count]
    group = math.gcd(8, *cuts)

    def kernel(*refs):
        refs = list(refs)
        table, pool_ref = (refs.pop(0) for _ in range(2))
        arrived_refs = [refs.pop(0) for _ in arrived]
        tile_refs = [[refs.pop(0) for _ in source] for source in tiles]
        bias = refs.pop(0)
        if target is not None:
            refs.pop(0)
        result = refs.pop(0)
        inputs = refs.pop(0) if fill else pool_ref
        outgoing = [] if final else [refs.pop(0) for _ in range(neigh)]
        in_sems = refs.pop(0)
        if final:
            outputs, out_sems = (refs.pop(0) for _ in range(2))
        if columns:
            inputs = refs.pop(0)

        def out_copy(part):
            here = outputs.at[:, pl.ds(part * group * width, group * width)]
            there = result.at[:, pl.ds((first + part * group) * width, group * width)]
            return pltpu.make_async_copy(here, there, out_sems.at[part])

        loads = []
        for slot, source in enumerate(arrived_refs):
            loads.append((source, inputs.at[blocks + slot]))
        if columns:
            for block in range(blocks):
                loads.append((pool_ref.at[:, pl.ds(block * width, width)], inputs.at[block]))
        loads = [pltpu.make_async_copy(*load, in_sems.at[place]) for place, load in enumerate(loads)]
        for copy in loads:
            copy.start()
        for copy in loads:
            copy.wait()

        def work(start, part, _):
            for g in range(group):
                block = part * group + g
                base = (layer * blocks + first + block) * fan
                weights = []
                for m in range(fan):
                    place, inside = places[m][start]
                    weights.append(tile_refs[m][place][block - start + inside])
                summed = jnp.dot(
                    jnp.concatenate([inputs[table[base + m]] for m in range(fan)], axis=1),
                    jnp.concatenate(weights, axis=0),
                    preferred_element_type=jnp.float32,
                )
                place = pl.multiple_of((first + block) * width, width)
                summed = summed + bias[layer : layer + 1, pl.ds(place, width)]
                summed = jnp.maximum(summed, 0.0).astype(result.dtype)
                if final:
                    outputs[:, pl.ds(pl.multiple_of(block * width, width), width)] = summed
                else:
                    result[first + block] = summed
            if final:
                out_copy(part).start()
            return _

        for start, end in zip(cuts, cuts[1:]):
            lax.fori_loop(start // group, end // group, functools.partial(work, start), None)
        for slot, there in enumerate(outgoing):
            there[...] = result[table[sends + slot]]
        if final:
            for part in range(count // group):
                out_copy(part).wait()

    anywhere = pl.BlockSpec(memory_space=pl.ANY)
    vmem, hbm = (pl.BlockSpec(memory_space=space) for space in (pltpu.VMEM, pltpu.HBM))
    neigh = NEIGH
    operands = [table, in_hbm(pool) if columns else in_vmem(pool), *arrived]
    in_specs = [hbm if columns else vmem] + [anywhere] * len(arrived)
    for source in tiles:
        operands += [in_vmem(array) for array in source]
        in_specs += [vmem] * len(source)
    operands.append(biases)
    in_specs.append(vmem)
    aliases = {}
    if target is not None:
        aliases[len(operands)] = 0
        operands.append(target)
        in_specs.append(anywhere)
    if final:
        out_shape, out_specs = [jax.ShapeDtypeStruct((rows, blocks * width), pool.dtype)], [anywhere]
    else:
        out_shape, out_specs = [pltpu.VMEM((blocks + neigh, rows, width), pool.dtype)], [vmem]
    if fill:
        aliases[1] = 1
        out_shape.append(pltpu.VMEM(pool.shape, pool.dtype))
        out_specs.append(vmem)
    if not final:
        out_shape += [jax.ShapeDtypeStruct((rows, width), pool.dtype)] * neigh
        out_specs += [vmem] * neigh
    scratch = [pltpu.SemaphoreType.DMA((blocks + neigh,))]
    if final:
        scratch += [pltpu.VMEM((rows, count * width), pool.dtype), pltpu.SemaphoreType.DMA((count // group,))]
    if columns:
        scratch.append(pltpu.VMEM((blocks + neigh, rows, width), pool.dtype))
    results = list(
        pl.pallas_call(
            kernel,
            out_shape=out_shape,
            grid_spec=pltpu.PrefetchScalarGridSpec(
                num_scalar_prefetch=1, in_specs=in_specs, out_specs=out_specs, scratch_shapes=scratch
            ),
            input_output_aliases=aliases,
            compiler_params=pltpu.CompilerParams(vmem_limit_bytes=LAYER_LIMIT),
            cost_estimate=FREE,
        )(*operands)
    )
    return results.pop(0), results.pop(0) if fill else pool, results


def body(activations, tile_weights, biases, source_codes, send_list):
    layer_count, block_count, part_rows, width = tile_weights.shape
    fan = source_codes.shape[2]
    part_count = lax.axis_size("dom")
    neighbor_offsets = (1, 2, -1, part_count // 2)
    sharers = width // part_rows
    own = lax.axis_index("batch") // sharers
    codes = jnp.take(source_codes, own ^ jnp.arange(fan), axis=2).reshape(-1)
    table = jnp.concatenate([codes, send_list.reshape(-1)])
    far = fan // 2
    unit = block_count // 16

    if sharers > 1:
        members = range(lax.axis_size("batch") // sharers)
        groups = [[m * sharers + s for s in range(sharers)] for m in members]
        tile_weights = lax.all_gather(tile_weights, "batch", axis=2, tiled=True, axis_index_groups=groups)

    def spread(held, first):
        for bit in range(far.bit_length() - 1):
            for m in range(1 << bit):
                held[first + m + (1 << bit)] = jax.tree.map(
                    lambda array: swapped(array, (1 << bit) * sharers), held[first + m]
                )

    last = layer_count - 1
    shares = [(0, (8, 8), (2, 2))] + [(layer, (16,), (4,)) for layer in range(1, last - 1)]
    shares += [(last - 1, (12, 4), (3, 1))]
    shares += [(last, (8, 4), (2, 2)), (last, (3, 1), (3, 1))]

    moves = {layer: [] for layer in range(layer_count)}
    for layer, sizes, _ in shares:
        for size in sizes:
            start = sum(count for _, _, count in moves[layer])
            moves[layer].append((layer, start, size * unit))
    mine = {layer: cut(tile_weights, moves[layer]) for layer in moves if layer}
    mine[0] = [cut(tile_weights, [move])[0] for move in moves[0]]
    crossed = {layer: [swapped(tile, far * sharers) for tile in mine[layer]] for layer in moves}

    whole = [tile_weights] + [None] * (fan - 1)
    spread(whole, 0)
    near = {layer: [cut(array, moves[layer]) for array in whole[1:far]] for layer in moves}

    current = activations
    outgoing = pick(table, codes.size, NEIGH, width, activations)
    before = None
    for layer, sizes, pieces in shares:
        if layer != before:
            arrived = [None] * NEIGH
            for turn, slot in enumerate(TURNS):
                block = outgoing[slot]
                if turn >= BOUNDARY:
                    block = lax.optimization_barrier((block, arrived[TURNS[turn - BOUNDARY]]))[0]
                arrived[slot] = shifted(block, "dom", neighbor_offsets[slot])
            pool, target, first, after = current, None, 0, arrived
        before = layer
        after = [*after, *(tile for source in near[layer] for tile in source)]
        tiles = [None] * fan
        for m, source in enumerate([mine[layer], *near[layer], crossed[layer]]):
            tiles[m] = [source.pop(0) for _ in sizes]
        for number, tile in zip(pieces, tiles[far]):
            tile = lax.optimization_barrier((tile, *after))[0]
            share = tile.shape[0] // math.gcd(number, tile.shape[0])
            passed = [None] * fan
            passed[far] = [tile[start : start + share] for start in range(0, tile.shape[0], share)]
            spread(passed, far)
            for m in range(far + 1, fan):
                tiles[m] = [*(tiles[m] or []), *passed[m]]
                after = [*after, *passed[m]]
        count = sum(sizes) * unit
        sends = codes.size + (layer + 1) * NEIGH
        target, pool, outgoing = run_blocks(
            layer, first, count, table, sends, pool, arrived, tiles, biases, target, layer == last
        )
        arrived = []
        current, first, after = target, first + count, [target]
    return current


def solution(mesh):
    in_specs = (
        P("batch", "dom"),
        P(None, "dom", "batch", None),
        P(None, "dom"),
        P(None, "dom", None),
        P(None, "dom", None),
    )
    out_specs = P("batch", "dom")
    return jax.shard_map(body, mesh=mesh, in_specs=in_specs, out_specs=out_specs, check_vma=False)
```

```python
import functools
import math

import jax
import jax.numpy as jnp
from jax import lax
from jax.experimental import pallas as pl
from jax.experimental.pallas import tpu as pltpu
from jax.sharding import PartitionSpec as P

TURNS = (3, 1, 0, 2)
BOUNDARY = 2
CUTS = 16
NEIGH = 4
VMEM_LIMIT = 16 * 2**20
LAYER_LIMIT = 20 * 2**20
FREE = pl.CostEstimate(flops=0, bytes_accessed=0, transcendentals=0)


def shifted(block, axis, distance):
    devices = range(lax.axis_size(axis))
    route = [((i - distance) % len(devices), i) for i in devices]
    return lax.ppermute(block, axis, route)


def swapped(block, mask):
    route = [(i, i ^ mask) for i in range(lax.axis_size("batch"))]
    return lax.ppermute(block, "batch", route)


def in_hbm(array):
    return pltpu.with_memory_space_constraint(array, pltpu.HBM)


def in_vmem(array):
    return pltpu.with_memory_space_constraint(array, pltpu.VMEM)


def cut(tile_weights, chunks):
    height, width = tile_weights.shape[2:]

    def kernel(tiles, *refs):
        targets, semaphores = refs[: len(chunks)], refs[len(chunks)]
        copies = []
        for place, (layer, first, count) in enumerate(chunks):
            step = count // math.gcd(CUTS, count)
            for part, start in enumerate(range(0, count, step)):
                source = tiles.at[layer, pl.ds(first + start, step)]
                there = targets[place].at[pl.ds(start, step)]
                copies.append(pltpu.make_async_copy(source, there, semaphores.at[place, part]))
        for copy in copies:
            copy.start()
        for copy in copies:
            copy.wait()

    parts = pl.pallas_call(
        kernel,
        out_shape=[pltpu.VMEM((count, height, width), tile_weights.dtype) for _, _, count in chunks],
        in_specs=[pl.BlockSpec(memory_space=pltpu.HBM)],
        out_specs=[pl.BlockSpec(memory_space=pltpu.VMEM)] * len(chunks),
        scratch_shapes=[pltpu.SemaphoreType.DMA((len(chunks), CUTS))],
        compiler_params=pltpu.CompilerParams(vmem_limit_bytes=VMEM_LIMIT),
        cost_estimate=FREE,
    )(in_hbm(tile_weights))
    return list(parts)


def pick(table, place, number, width, activations):
    rows = activations.shape[0]

    def kernel(table, source, *refs):
        targets, semaphores = refs[:number], refs[number]
        copies = []
        for slot in range(number):
            start = pl.multiple_of(table[place + slot] * width, width)
            copies.append(pltpu.make_async_copy(source.at[:, pl.ds(start, width)], targets[slot], semaphores.at[slot]))
        for copy in copies:
            copy.start()
        for copy in copies:
            copy.wait()

    return pl.pallas_call(
        kernel,
        out_shape=[jax.ShapeDtypeStruct((rows, width), activations.dtype)] * number,
        grid_spec=pltpu.PrefetchScalarGridSpec(
            num_scalar_prefetch=1,
            in_specs=[pl.BlockSpec(memory_space=pltpu.HBM)],
            out_specs=[pl.BlockSpec(memory_space=pltpu.VMEM)] * number,
            scratch_shapes=[pltpu.SemaphoreType.DMA((number,))],
        ),
        compiler_params=pltpu.CompilerParams(vmem_limit_bytes=VMEM_LIMIT),
        cost_estimate=FREE,
    )(table, in_hbm(activations))


def run_blocks(layer, first, count, table, sends, pool, arrived, tiles, biases, target, final):
    fan, width = len(tiles), tiles[0][0].shape[2]
    rows, blocks = pool.shape[-2], biases.shape[1] // width
    columns = pool.ndim == 2
    fill = bool(arrived) and not columns
    places = {}
    for m in range(fan):
        places[m] = [(part, inside) for part, array in enumerate(tiles[m]) for inside in range(array.shape[0])]
    cuts = [block for block in range(count) if any(places[m][block][1] == 0 for m in range(fan))] + [count]
    group = math.gcd(8, *cuts)

    def kernel(*refs):
        refs = list(refs)
        table, pool_ref = (refs.pop(0) for _ in range(2))
        arrived_refs = [refs.pop(0) for _ in arrived]
        tile_refs = [[refs.pop(0) for _ in source] for source in tiles]
        bias = refs.pop(0)
        if target is not None:
            refs.pop(0)
        result = refs.pop(0)
        inputs = refs.pop(0) if fill else pool_ref
        outgoing = [] if final else [refs.pop(0) for _ in range(neigh)]
        in_sems = refs.pop(0)
        if final:
            outputs, out_sems = (refs.pop(0) for _ in range(2))
        if columns:
            inputs = refs.pop(0)

        def out_copy(part):
            here = outputs.at[:, pl.ds(part * group * width, group * width)]
            there = result.at[:, pl.ds((first + part * group) * width, group * width)]
            return pltpu.make_async_copy(here, there, out_sems.at[part])

        loads = []
        for slot, source in enumerate(arrived_refs):
            loads.append((source, inputs.at[blocks + slot]))
        if columns:
            for block in range(blocks):
                loads.append((pool_ref.at[:, pl.ds(block * width, width)], inputs.at[block]))
        loads = [pltpu.make_async_copy(*load, in_sems.at[place]) for place, load in enumerate(loads)]
        for copy in loads:
            copy.start()
        for copy in loads:
            copy.wait()

        def work(start, part, _):
            for g in range(group):
                block = part * group + g
                base = (layer * blocks + first + block) * fan
                weights = []
                for m in range(fan):
                    place, inside = places[m][start]
                    weights.append(tile_refs[m][place][block - start + inside])
                summed = jnp.dot(
                    jnp.concatenate([inputs[table[base + m]] for m in range(fan)], axis=1),
                    jnp.concatenate(weights, axis=0),
                    preferred_element_type=jnp.float32,
                )
                place = pl.multiple_of((first + block) * width, width)
                summed = summed + bias[layer : layer + 1, pl.ds(place, width)]
                summed = jnp.maximum(summed, 0.0).astype(result.dtype)
                if final:
                    outputs[:, pl.ds(pl.multiple_of(block * width, width), width)] = summed
                else:
                    result[first + block] = summed
            if final:
                out_copy(part).start()
            return _

        for start, end in zip(cuts, cuts[1:]):
            lax.fori_loop(start // group, end // group, functools.partial(work, start), None)
        for slot, there in enumerate(outgoing):
            there[...] = result[table[sends + slot]]
        if final:
            for part in range(count // group):
                out_copy(part).wait()

    anywhere = pl.BlockSpec(memory_space=pl.ANY)
    vmem, hbm = (pl.BlockSpec(memory_space=space) for space in (pltpu.VMEM, pltpu.HBM))
    neigh = NEIGH
    operands = [table, in_hbm(pool) if columns else in_vmem(pool), *arrived]
    in_specs = [hbm if columns else vmem] + [anywhere] * len(arrived)
    for source in tiles:
        operands += [in_vmem(array) for array in source]
        in_specs += [vmem] * len(source)
    operands.append(biases)
    in_specs.append(vmem)
    aliases = {}
    if target is not None:
        aliases[len(operands)] = 0
        operands.append(target)
        in_specs.append(anywhere)
    if final:
        out_shape, out_specs = [jax.ShapeDtypeStruct((rows, blocks * width), pool.dtype)], [anywhere]
    else:
        out_shape, out_specs = [pltpu.VMEM((blocks + neigh, rows, width), pool.dtype)], [vmem]
    if fill:
        aliases[1] = 1
        out_shape.append(pltpu.VMEM(pool.shape, pool.dtype))
        out_specs.append(vmem)
    if not final:
        out_shape += [jax.ShapeDtypeStruct((rows, width), pool.dtype)] * neigh
        out_specs += [vmem] * neigh
    scratch = [pltpu.SemaphoreType.DMA((blocks + neigh,))]
    if final:
        scratch += [pltpu.VMEM((rows, count * width), pool.dtype), pltpu.SemaphoreType.DMA((count // group,))]
    if columns:
        scratch.append(pltpu.VMEM((blocks + neigh, rows, width), pool.dtype))
    results = list(
        pl.pallas_call(
            kernel,
            out_shape=out_shape,
            grid_spec=pltpu.PrefetchScalarGridSpec(
                num_scalar_prefetch=1, in_specs=in_specs, out_specs=out_specs, scratch_shapes=scratch
            ),
            input_output_aliases=aliases,
            compiler_params=pltpu.CompilerParams(vmem_limit_bytes=LAYER_LIMIT),
            cost_estimate=FREE,
        )(*operands)
    )
    return results.pop(0), results.pop(0) if fill else pool, results


def body(activations, tile_weights, biases, source_codes, send_list):
    layer_count, block_count, part_rows, width = tile_weights.shape
    fan = source_codes.shape[2]
    part_count = lax.axis_size("dom")
    neighbor_offsets = (1, 2, -1, part_count // 2)
    sharers = width // part_rows
    own = lax.axis_index("batch") // sharers
    codes = jnp.take(source_codes, own ^ jnp.arange(fan), axis=2).reshape(-1)
    table = jnp.concatenate([codes, send_list.reshape(-1)])
    far = fan // 2
    unit = block_count // 16

    if sharers > 1:
        members = range(lax.axis_size("batch") // sharers)
        groups = [[m * sharers + s for s in range(sharers)] for m in members]
        tile_weights = lax.all_gather(tile_weights, "batch", axis=2, tiled=True, axis_index_groups=groups)

    def spread(held, first):
        for bit in range(far.bit_length() - 1):
            for m in range(1 << bit):
                held[first + m + (1 << bit)] = jax.tree.map(
                    lambda array: swapped(array, (1 << bit) * sharers), held[first + m]
                )

    last = layer_count - 1
    shares = [(0, (8, 8), ((4, 4), (4, 4)))]
    shares += [(layer, (16,), ((4, 4, 4, 4),)) for layer in range(1, last - 1)]
    shares += [(last - 1, (12, 4), ((4, 4, 4), (4,)))]
    shares += [(last, (8,), ((4, 4),)), (last, (5,), ((2, 2, 1),)), (last, (3,), ((2, 1),))]

    moves = {layer: [] for layer in range(layer_count)}
    for layer, sizes, _ in shares:
        for size in sizes:
            start = sum(count for _, _, count in moves[layer])
            moves[layer].append((layer, start, size * unit))
    mine = {layer: cut(tile_weights, moves[layer]) for layer in moves if layer}
    mine[0] = [cut(tile_weights, [move])[0] for move in moves[0]]
    crossed = {layer: [swapped(tile, far * sharers) for tile in mine[layer]] for layer in moves}

    whole = [tile_weights] + [None] * (fan - 1)
    spread(whole, 0)
    near = {layer: [cut(array, moves[layer]) for array in whole[1:far]] for layer in moves}

    current = activations
    outgoing = pick(table, codes.size, NEIGH, width, activations)
    before = None
    for layer, sizes, pieces in shares:
        if layer != before:
            arrived = [None] * NEIGH
            for turn, slot in enumerate(TURNS):
                block = outgoing[slot]
                if turn >= BOUNDARY:
                    block = lax.optimization_barrier((block, arrived[TURNS[turn - BOUNDARY]]))[0]
                arrived[slot] = shifted(block, "dom", neighbor_offsets[slot])
            pool, target, first, after = current, None, 0, arrived
        before = layer
        after = [*after, *(tile for source in near[layer] for tile in source)]
        tiles = [None] * fan
        for m, source in enumerate([mine[layer], *near[layer], crossed[layer]]):
            tiles[m] = [source.pop(0) for _ in sizes]
        for parts, tile in zip(pieces, tiles[far]):
            tile = lax.optimization_barrier((tile, *after))[0]
            passed = [None] * fan
            starts = [sum(parts[:place]) * unit for place in range(len(parts) + 1)]
            passed[far] = [tile[start:end] for start, end in zip(starts, starts[1:])]
            spread(passed, far)
            for m in range(far + 1, fan):
                tiles[m] = [*(tiles[m] or []), *passed[m]]
                after = [*after, *passed[m]]
        count = sum(sizes) * unit
        sends = codes.size + (layer + 1) * NEIGH
        target, pool, outgoing = run_blocks(
            layer, first, count, table, sends, pool, arrived, tiles, biases, target, layer == last
        )
        arrived = []
        current, first, after = target, first + count, [target]
    return current


def solution(mesh):
    in_specs = (
        P("batch", "dom"),
        P(None, "dom", "batch", None),
        P(None, "dom"),
        P(None, "dom", None),
        P(None, "dom", None),
    )
    out_specs = P("batch", "dom")
    return jax.shard_map(body, mesh=mesh, in_specs=in_specs, out_specs=out_specs, check_vma=False)
```

```python
import functools
import math

import jax
import jax.numpy as jnp
from jax import lax
from jax.experimental import pallas as pl
from jax.experimental.pallas import tpu as pltpu
from jax.sharding import PartitionSpec as P

TURNS = (3, 1, 0, 2)
BOUNDARY = 2
CUTS = 16
NEIGH = 4
VMEM_LIMIT = 16 * 2**20
LAYER_LIMIT = 20 * 2**20
FREE = pl.CostEstimate(flops=0, bytes_accessed=0, transcendentals=0)


def shifted(block, axis, distance):
    devices = range(lax.axis_size(axis))
    route = [((i - distance) % len(devices), i) for i in devices]
    return lax.ppermute(block, axis, route)


def swapped(block, mask):
    route = [(i, i ^ mask) for i in range(lax.axis_size("batch"))]
    return lax.ppermute(block, "batch", route)


def in_hbm(array):
    return pltpu.with_memory_space_constraint(array, pltpu.HBM)


def in_vmem(array):
    return pltpu.with_memory_space_constraint(array, pltpu.VMEM)


def cut(tile_weights, chunks):
    height, width = tile_weights.shape[2:]

    def kernel(tiles, *refs):
        targets, semaphores = refs[: len(chunks)], refs[len(chunks)]
        copies = []
        for place, (layer, first, count) in enumerate(chunks):
            step = count // math.gcd(CUTS, count)
            for part, start in enumerate(range(0, count, step)):
                source = tiles.at[layer, pl.ds(first + start, step)]
                there = targets[place].at[pl.ds(start, step)]
                copies.append(pltpu.make_async_copy(source, there, semaphores.at[place, part]))
        for copy in copies:
            copy.start()
        for copy in copies:
            copy.wait()

    parts = pl.pallas_call(
        kernel,
        out_shape=[pltpu.VMEM((count, height, width), tile_weights.dtype) for _, _, count in chunks],
        in_specs=[pl.BlockSpec(memory_space=pltpu.HBM)],
        out_specs=[pl.BlockSpec(memory_space=pltpu.VMEM)] * len(chunks),
        scratch_shapes=[pltpu.SemaphoreType.DMA((len(chunks), CUTS))],
        compiler_params=pltpu.CompilerParams(vmem_limit_bytes=VMEM_LIMIT),
        cost_estimate=FREE,
    )(in_hbm(tile_weights))
    return list(parts)


def pick(table, place, number, width, activations):
    rows = activations.shape[0]

    def kernel(table, source, *refs):
        targets, semaphores = refs[:number], refs[number]
        copies = []
        for slot in range(number):
            start = pl.multiple_of(table[place + slot] * width, width)
            copies.append(pltpu.make_async_copy(source.at[:, pl.ds(start, width)], targets[slot], semaphores.at[slot]))
        for copy in copies:
            copy.start()
        for copy in copies:
            copy.wait()

    return pl.pallas_call(
        kernel,
        out_shape=[jax.ShapeDtypeStruct((rows, width), activations.dtype)] * number,
        grid_spec=pltpu.PrefetchScalarGridSpec(
            num_scalar_prefetch=1,
            in_specs=[pl.BlockSpec(memory_space=pltpu.HBM)],
            out_specs=[pl.BlockSpec(memory_space=pltpu.VMEM)] * number,
            scratch_shapes=[pltpu.SemaphoreType.DMA((number,))],
        ),
        compiler_params=pltpu.CompilerParams(vmem_limit_bytes=VMEM_LIMIT),
        cost_estimate=FREE,
    )(table, in_hbm(activations))


def run_blocks(layer, first, count, table, sends, pool, arrived, tiles, biases, target, final):
    fan, width = len(tiles), tiles[0][0].shape[2]
    rows, blocks = pool.shape[-2], biases.shape[1] // width
    columns = pool.ndim == 2
    fill = bool(arrived) and not columns
    places = {}
    for m in range(fan):
        places[m] = [(part, inside) for part, array in enumerate(tiles[m]) for inside in range(array.shape[0])]
    cuts = [block for block in range(count) if any(places[m][block][1] == 0 for m in range(fan))] + [count]
    group = math.gcd(8, *cuts)

    def kernel(*refs):
        refs = list(refs)
        table, pool_ref = (refs.pop(0) for _ in range(2))
        arrived_refs = [refs.pop(0) for _ in arrived]
        tile_refs = [[refs.pop(0) for _ in source] for source in tiles]
        bias = refs.pop(0)
        if target is not None:
            refs.pop(0)
        result = refs.pop(0)
        inputs = refs.pop(0) if fill else pool_ref
        outgoing = [] if final else [refs.pop(0) for _ in range(neigh)]
        in_sems = refs.pop(0)
        if final:
            outputs, out_sems = (refs.pop(0) for _ in range(2))
        if columns:
            inputs = refs.pop(0)

        def out_copy(part):
            here = outputs.at[:, pl.ds(part * group * width, group * width)]
            there = result.at[:, pl.ds((first + part * group) * width, group * width)]
            return pltpu.make_async_copy(here, there, out_sems.at[part])

        loads = []
        for slot, source in enumerate(arrived_refs):
            loads.append((source, inputs.at[blocks + slot]))
        if columns:
            for block in range(blocks):
                loads.append((pool_ref.at[:, pl.ds(block * width, width)], inputs.at[block]))
        loads = [pltpu.make_async_copy(*load, in_sems.at[place]) for place, load in enumerate(loads)]
        for copy in loads:
            copy.start()
        for copy in loads:
            copy.wait()

        def work(start, part, _):
            for g in range(group):
                block = part * group + g
                base = (layer * blocks + first + block) * fan
                weights = []
                for m in range(fan):
                    place, inside = places[m][start]
                    weights.append(tile_refs[m][place][block - start + inside])
                summed = jnp.dot(
                    jnp.concatenate([inputs[table[base + m]] for m in range(fan)], axis=1),
                    jnp.concatenate(weights, axis=0),
                    preferred_element_type=jnp.float32,
                )
                place = pl.multiple_of((first + block) * width, width)
                summed = summed + bias[layer : layer + 1, pl.ds(place, width)]
                summed = jnp.maximum(summed, 0.0).astype(result.dtype)
                if final:
                    outputs[:, pl.ds(pl.multiple_of(block * width, width), width)] = summed
                else:
                    result[first + block] = summed
            if final:
                out_copy(part).start()
            return _

        for start, end in zip(cuts, cuts[1:]):
            lax.fori_loop(start // group, end // group, functools.partial(work, start), None)
        for slot, there in enumerate(outgoing):
            there[...] = result[table[sends + slot]]
        if final:
            for part in range(count // group):
                out_copy(part).wait()

    anywhere = pl.BlockSpec(memory_space=pl.ANY)
    vmem, hbm = (pl.BlockSpec(memory_space=space) for space in (pltpu.VMEM, pltpu.HBM))
    neigh = NEIGH
    operands = [table, in_hbm(pool) if columns else in_vmem(pool), *arrived]
    in_specs = [hbm if columns else vmem] + [anywhere] * len(arrived)
    for source in tiles:
        operands += [in_vmem(array) for array in source]
        in_specs += [vmem] * len(source)
    operands.append(biases)
    in_specs.append(vmem)
    aliases = {}
    if target is not None:
        aliases[len(operands)] = 0
        operands.append(target)
        in_specs.append(anywhere)
    if final:
        out_shape, out_specs = [jax.ShapeDtypeStruct((rows, blocks * width), pool.dtype)], [anywhere]
    else:
        out_shape, out_specs = [pltpu.VMEM((blocks + neigh, rows, width), pool.dtype)], [vmem]
    if fill:
        aliases[1] = 1
        out_shape.append(pltpu.VMEM(pool.shape, pool.dtype))
        out_specs.append(vmem)
    if not final:
        out_shape += [jax.ShapeDtypeStruct((rows, width), pool.dtype)] * neigh
        out_specs += [vmem] * neigh
    scratch = [pltpu.SemaphoreType.DMA((len(arrived) + (blocks if columns else 0) or 1,))]
    if final:
        scratch += [pltpu.VMEM((rows, count * width), pool.dtype), pltpu.SemaphoreType.DMA((count // group,))]
    if columns:
        scratch.append(pltpu.VMEM((blocks + neigh, rows, width), pool.dtype))
    results = list(
        pl.pallas_call(
            kernel,
            out_shape=out_shape,
            grid_spec=pltpu.PrefetchScalarGridSpec(
                num_scalar_prefetch=1, in_specs=in_specs, out_specs=out_specs, scratch_shapes=scratch
            ),
            input_output_aliases=aliases,
            compiler_params=pltpu.CompilerParams(vmem_limit_bytes=LAYER_LIMIT),
            cost_estimate=FREE,
        )(*operands)
    )
    return results.pop(0), results.pop(0) if fill else pool, results


def body(activations, tile_weights, biases, source_codes, send_list):
    layer_count, block_count, part_rows, width = tile_weights.shape
    fan = source_codes.shape[2]
    part_count = lax.axis_size("dom")
    neighbor_offsets = (1, 2, -1, part_count // 2)
    sharers = width // part_rows
    own = lax.axis_index("batch") // sharers
    codes = jnp.take(source_codes, own ^ jnp.arange(fan), axis=2).reshape(-1)
    table = jnp.concatenate([codes, send_list.reshape(-1)])
    far = fan // 2
    unit = block_count // 16

    if sharers > 1:
        members = range(lax.axis_size("batch") // sharers)
        groups = [[m * sharers + s for s in range(sharers)] for m in members]
        tile_weights = lax.all_gather(tile_weights, "batch", axis=2, tiled=True, axis_index_groups=groups)

    def spread(held, first):
        for bit in range(far.bit_length() - 1):
            for m in range(1 << bit):
                held[first + m + (1 << bit)] = jax.tree.map(
                    lambda array: swapped(array, (1 << bit) * sharers), held[first + m]
                )

    last = layer_count - 1
    shares = [(0, (8, 8), ((4, 4), (4, 4))), (1, (8, 8), ((4, 4), (4, 4))), (2, (8, 8), ((4, 4), (4, 4))), (last, (8,), ((4, 4),)), (last, (5,), ((2, 2, 1),)), (last, (3,), ((3,),))]

    moves = {layer: [] for layer in range(layer_count)}
    for layer, sizes, _ in shares:
        for size in sizes:
            start = sum(count for _, _, count in moves[layer])
            moves[layer].append((layer, start, size * unit))
    mine = {layer: cut(tile_weights, moves[layer]) for layer in moves if layer}
    mine[0] = [cut(tile_weights, [move])[0] for move in moves[0]]
    crossed = {layer: [swapped(tile, far * sharers) for tile in mine[layer]] for layer in moves}

    whole = [tile_weights] + [None] * (fan - 1)
    spread(whole, 0)
    near = {layer: [cut(array, moves[layer]) for array in whole[1:far]] for layer in moves}

    current = activations
    outgoing = pick(table, codes.size, NEIGH, width, activations)
    before = None
    for layer, sizes, pieces in shares:
        if layer != before:
            arrived = [None] * NEIGH
            for turn, slot in enumerate(TURNS):
                block = outgoing[slot]
                if turn >= BOUNDARY:
                    block = lax.optimization_barrier((block, arrived[TURNS[turn - BOUNDARY]]))[0]
                arrived[slot] = shifted(block, "dom", neighbor_offsets[slot])
            pool, target, first, after = current, None, 0, arrived
        before = layer
        after = [*after, *(tile for source in near[layer] for tile in source)]
        tiles = [None] * fan
        for m, source in enumerate([mine[layer], *near[layer], crossed[layer]]):
            tiles[m] = [source.pop(0) for _ in sizes]
        for parts, tile in zip(pieces, tiles[far]):
            tile = lax.optimization_barrier((tile, *after))[0]
            passed = [None] * fan
            starts = [sum(parts[:place]) * unit for place in range(len(parts) + 1)]
            passed[far] = [tile[start:end] for start, end in zip(starts, starts[1:])]
            spread(passed, far)
            for m in range(far + 1, fan):
                tiles[m] = [*(tiles[m] or []), *passed[m]]
                after = [*after, *passed[m]]
        count = sum(sizes) * unit
        sends = codes.size + (layer + 1) * NEIGH
        target, pool, outgoing = run_blocks(
            layer, first, count, table, sends, pool, arrived, tiles, biases, target, layer == last
        )
        arrived = []
        current, first, after = target, first + count, [target]
    return current


def solution(mesh):
    in_specs = (
        P("batch", "dom"),
        P(None, "dom", "batch", None),
        P(None, "dom"),
        P(None, "dom", None),
        P(None, "dom", None),
    )
    out_specs = P("batch", "dom")
    return jax.shard_map(body, mesh=mesh, in_specs=in_specs, out_specs=out_specs, check_vma=False)
```

```python
import functools
import math

import jax
import jax.numpy as jnp
from jax import lax
from jax.experimental import pallas as pl
from jax.experimental.pallas import tpu as pltpu
from jax.sharding import PartitionSpec as P

TURNS = (3, 1, 0, 2)
BOUNDARY = 2
CUTS = 16
NEIGH = 4
VMEM_LIMIT = 16 * 2**20
LAYER_LIMIT = 20 * 2**20
FREE = pl.CostEstimate(flops=0, bytes_accessed=0, transcendentals=0)


def shifted(block, axis, distance):
    devices = range(lax.axis_size(axis))
    route = [((i - distance) % len(devices), i) for i in devices]
    return lax.ppermute(block, axis, route)


def swapped(block, mask):
    route = [(i, i ^ mask) for i in range(lax.axis_size("batch"))]
    return lax.ppermute(block, "batch", route)


def in_hbm(array):
    return pltpu.with_memory_space_constraint(array, pltpu.HBM)


def in_vmem(array):
    return pltpu.with_memory_space_constraint(array, pltpu.VMEM)


def cut(tile_weights, chunks):
    height, width = tile_weights.shape[2:]

    def kernel(tiles, *refs):
        targets, semaphores = refs[: len(chunks)], refs[len(chunks)]
        copies = []
        for place, (layer, first, count) in enumerate(chunks):
            step = count // math.gcd(CUTS, count)
            for part, start in enumerate(range(0, count, step)):
                source = tiles.at[layer, pl.ds(first + start, step)]
                there = targets[place].at[pl.ds(start, step)]
                copies.append(pltpu.make_async_copy(source, there, semaphores.at[place, part]))
        for copy in copies:
            copy.start()
        for copy in copies:
            copy.wait()

    parts = pl.pallas_call(
        kernel,
        out_shape=[pltpu.VMEM((count, height, width), tile_weights.dtype) for _, _, count in chunks],
        in_specs=[pl.BlockSpec(memory_space=pltpu.HBM)],
        out_specs=[pl.BlockSpec(memory_space=pltpu.VMEM)] * len(chunks),
        scratch_shapes=[pltpu.SemaphoreType.DMA((len(chunks), CUTS))],
        compiler_params=pltpu.CompilerParams(vmem_limit_bytes=VMEM_LIMIT),
        cost_estimate=FREE,
    )(in_hbm(tile_weights))
    return list(parts)


def pick(table, place, number, width, activations):
    rows = activations.shape[0]

    def kernel(table, source, *refs):
        targets, semaphores = refs[:number], refs[number]
        copies = []
        for slot in range(number):
            start = pl.multiple_of(table[place + slot] * width, width)
            copies.append(pltpu.make_async_copy(source.at[:, pl.ds(start, width)], targets[slot], semaphores.at[slot]))
        for copy in copies:
            copy.start()
        for copy in copies:
            copy.wait()

    return pl.pallas_call(
        kernel,
        out_shape=[jax.ShapeDtypeStruct((rows, width), activations.dtype)] * number,
        grid_spec=pltpu.PrefetchScalarGridSpec(
            num_scalar_prefetch=1,
            in_specs=[pl.BlockSpec(memory_space=pltpu.HBM)],
            out_specs=[pl.BlockSpec(memory_space=pltpu.VMEM)] * number,
            scratch_shapes=[pltpu.SemaphoreType.DMA((number,))],
        ),
        compiler_params=pltpu.CompilerParams(vmem_limit_bytes=VMEM_LIMIT),
        cost_estimate=FREE,
    )(table, in_hbm(activations))


def run_blocks(layer, first, count, table, sends, pool, arrived, tiles, biases, target, final):
    fan, width = len(tiles), tiles[0][0].shape[2]
    rows, blocks = pool.shape[-2], biases.shape[1] // width
    columns = pool.ndim == 2
    fill = bool(arrived) and not columns
    places = {}
    for m in range(fan):
        places[m] = [(part, inside) for part, array in enumerate(tiles[m]) for inside in range(array.shape[0])]
    cuts = [block for block in range(count) if any(places[m][block][1] == 0 for m in range(fan))] + [count]
    group = math.gcd(8, *cuts)

    def kernel(*refs):
        refs = list(refs)
        table, pool_ref = (refs.pop(0) for _ in range(2))
        arrived_refs = [refs.pop(0) for _ in arrived]
        tile_refs = [[refs.pop(0) for _ in source] for source in tiles]
        bias = refs.pop(0)
        if target is not None:
            refs.pop(0)
        result = refs.pop(0)
        inputs = refs.pop(0) if fill else pool_ref
        outgoing = [] if final else [refs.pop(0) for _ in range(neigh)]
        in_sems = refs.pop(0)
        if final:
            outputs, out_sems = (refs.pop(0) for _ in range(2))
        if columns:
            inputs = refs.pop(0)

        def out_copy(part):
            here = outputs.at[:, pl.ds(part * group * width, group * width)]
            there = result.at[:, pl.ds((first + part * group) * width, group * width)]
            return pltpu.make_async_copy(here, there, out_sems.at[part])

        loads = []
        for slot, source in enumerate(arrived_refs):
            loads.append((source, inputs.at[blocks + slot]))
        if columns:
            for block in range(blocks):
                loads.append((pool_ref.at[:, pl.ds(block * width, width)], inputs.at[block]))
        loads = [pltpu.make_async_copy(*load, in_sems.at[place]) for place, load in enumerate(loads)]
        for copy in loads:
            copy.start()
        for copy in loads:
            copy.wait()

        def work(start, part, _):
            for g in range(group):
                block = part * group + g
                base = (layer * blocks + first + block) * fan
                weights = []
                for m in range(fan):
                    place, inside = places[m][start]
                    weights.append(tile_refs[m][place][block - start + inside])
                summed = jnp.dot(
                    jnp.concatenate([inputs[table[base + m]] for m in range(fan)], axis=1),
                    jnp.concatenate(weights, axis=0),
                    preferred_element_type=jnp.float32,
                )
                place = pl.multiple_of((first + block) * width, width)
                summed = summed + bias[layer : layer + 1, pl.ds(place, width)]
                summed = jnp.maximum(summed, 0.0).astype(result.dtype)
                if final:
                    outputs[:, pl.ds(pl.multiple_of(block * width, width), width)] = summed
                else:
                    result[first + block] = summed
            if final:
                out_copy(part).start()
            return _

        for start, end in zip(cuts, cuts[1:]):
            turns = (end - start) // group
            lax.fori_loop(start // group, end // group, functools.partial(work, start), None, unroll=turns if final else 1)
        for slot, there in enumerate(outgoing):
            there[...] = result[table[sends + slot]]
        if final:
            for part in range(count // group):
                out_copy(part).wait()

    anywhere = pl.BlockSpec(memory_space=pl.ANY)
    vmem, hbm = (pl.BlockSpec(memory_space=space) for space in (pltpu.VMEM, pltpu.HBM))
    neigh = NEIGH
    operands = [table, in_hbm(pool) if columns else in_vmem(pool), *arrived]
    in_specs = [hbm if columns else vmem] + [anywhere] * len(arrived)
    for source in tiles:
        operands += [in_vmem(array) for array in source]
        in_specs += [vmem] * len(source)
    operands.append(biases)
    in_specs.append(vmem)
    aliases = {}
    if target is not None:
        aliases[len(operands)] = 0
        operands.append(target)
        in_specs.append(anywhere)
    if final:
        out_shape, out_specs = [jax.ShapeDtypeStruct((rows, blocks * width), pool.dtype)], [anywhere]
    else:
        out_shape, out_specs = [pltpu.VMEM((blocks + neigh, rows, width), pool.dtype)], [vmem]
    if fill:
        aliases[1] = 1
        out_shape.append(pltpu.VMEM(pool.shape, pool.dtype))
        out_specs.append(vmem)
    if not final:
        out_shape += [jax.ShapeDtypeStruct((rows, width), pool.dtype)] * neigh
        out_specs += [vmem] * neigh
    scratch = [pltpu.SemaphoreType.DMA((len(arrived) + (blocks if columns else 0) or 1,))]
    if final:
        scratch += [pltpu.VMEM((rows, count * width), pool.dtype), pltpu.SemaphoreType.DMA((count // group,))]
    if columns:
        scratch.append(pltpu.VMEM((blocks + neigh, rows, width), pool.dtype))
    results = list(
        pl.pallas_call(
            kernel,
            out_shape=out_shape,
            grid_spec=pltpu.PrefetchScalarGridSpec(
                num_scalar_prefetch=1, in_specs=in_specs, out_specs=out_specs, scratch_shapes=scratch
            ),
            input_output_aliases=aliases,
            compiler_params=pltpu.CompilerParams(vmem_limit_bytes=LAYER_LIMIT),
            cost_estimate=FREE,
        )(*operands)
    )
    return results.pop(0), results.pop(0) if fill else pool, results


def body(activations, tile_weights, biases, source_codes, send_list):
    layer_count, block_count, part_rows, width = tile_weights.shape
    fan = source_codes.shape[2]
    part_count = lax.axis_size("dom")
    neighbor_offsets = (1, 2, -1, part_count // 2)
    sharers = width // part_rows
    own = lax.axis_index("batch") // sharers
    codes = jnp.take(source_codes, own ^ jnp.arange(fan), axis=2).reshape(-1)
    table = jnp.concatenate([codes, send_list.reshape(-1)])
    far = fan // 2
    unit = block_count // 16

    if sharers > 1:
        members = range(lax.axis_size("batch") // sharers)
        groups = [[m * sharers + s for s in range(sharers)] for m in members]
        tile_weights = lax.all_gather(tile_weights, "batch", axis=2, tiled=True, axis_index_groups=groups)

    def spread(held, first):
        for bit in range(far.bit_length() - 1):
            for m in range(1 << bit):
                held[first + m + (1 << bit)] = jax.tree.map(
                    lambda array: swapped(array, (1 << bit) * sharers), held[first + m]
                )

    last = layer_count - 1
    shares = [(0, (8, 8), ((4, 4), (4, 4))), (1, (8, 8), ((4, 4), (4, 4))), (2, (8, 8), ((4, 4), (4, 4))), (last, (8,), ((4, 4),)), (last, (5,), ((2, 2, 1),)), (last, (3,), ((3,),))]

    moves = {layer: [] for layer in range(layer_count)}
    for layer, sizes, _ in shares:
        for size in sizes:
            start = sum(count for _, _, count in moves[layer])
            moves[layer].append((layer, start, size * unit))
    mine = {layer: cut(tile_weights, moves[layer]) for layer in moves if layer}
    mine[0] = [cut(tile_weights, [move])[0] for move in moves[0]]
    crossed = {layer: [swapped(tile, far * sharers) for tile in mine[layer]] for layer in moves}

    whole = [tile_weights] + [None] * (fan - 1)
    spread(whole, 0)
    near = {layer: [cut(array, moves[layer]) for array in whole[1:far]] for layer in moves}

    current = activations
    outgoing = pick(table, codes.size, NEIGH, width, activations)
    before = None
    for layer, sizes, pieces in shares:
        if layer != before:
            arrived = [None] * NEIGH
            for turn, slot in enumerate(TURNS):
                block = outgoing[slot]
                if turn >= BOUNDARY:
                    block = lax.optimization_barrier((block, arrived[TURNS[turn - BOUNDARY]]))[0]
                arrived[slot] = shifted(block, "dom", neighbor_offsets[slot])
            pool, target, first, after = current, None, 0, arrived
        before = layer
        after = [*after, *(tile for source in near[layer] for tile in source)]
        tiles = [None] * fan
        for m, source in enumerate([mine[layer], *near[layer], crossed[layer]]):
            tiles[m] = [source.pop(0) for _ in sizes]
        for parts, tile in zip(pieces, tiles[far]):
            tile = lax.optimization_barrier((tile, *after))[0]
            passed = [None] * fan
            starts = [sum(parts[:place]) * unit for place in range(len(parts) + 1)]
            passed[far] = [tile[start:end] for start, end in zip(starts, starts[1:])]
            spread(passed, far)
            for m in range(far + 1, fan):
                tiles[m] = [*(tiles[m] or []), *passed[m]]
                after = [*after, *passed[m]]
        count = sum(sizes) * unit
        sends = codes.size + (layer + 1) * NEIGH
        target, pool, outgoing = run_blocks(
            layer, first, count, table, sends, pool, arrived, tiles, biases, target, layer == last
        )
        arrived = []
        current, first, after = target, first + count, [target]
    return current


def solution(mesh):
    in_specs = (
        P("batch", "dom"),
        P(None, "dom", "batch", None),
        P(None, "dom"),
        P(None, "dom", None),
        P(None, "dom", None),
    )
    out_specs = P("batch", "dom")
    return jax.shard_map(body, mesh=mesh, in_specs=in_specs, out_specs=out_specs, check_vma=False)
```

```python
import functools
import math

import jax
import jax.numpy as jnp
from jax import lax
from jax.experimental import pallas as pl
from jax.experimental.pallas import tpu as pltpu
from jax.sharding import PartitionSpec as P

TURNS = (3, 1, 0, 2)
BOUNDARY = 2
CUTS = 16
NEIGH = 4
VMEM_LIMIT = 16 * 2**20
LAYER_LIMIT = 20 * 2**20
FREE = pl.CostEstimate(flops=0, bytes_accessed=0, transcendentals=0)


def shifted(block, axis, distance):
    devices = range(lax.axis_size(axis))
    route = [((i - distance) % len(devices), i) for i in devices]
    return lax.ppermute(block, axis, route)


def swapped(block, mask):
    route = [(i, i ^ mask) for i in range(lax.axis_size("batch"))]
    return lax.ppermute(block, "batch", route)


def in_hbm(array):
    return pltpu.with_memory_space_constraint(array, pltpu.HBM)


def in_vmem(array):
    return pltpu.with_memory_space_constraint(array, pltpu.VMEM)


def cut(tile_weights, chunks):
    height, width = tile_weights.shape[2:]

    def kernel(tiles, *refs):
        targets, semaphores = refs[: len(chunks)], refs[len(chunks)]
        copies = []
        for place, (layer, first, count) in enumerate(chunks):
            step = count // math.gcd(CUTS, count)
            for part, start in enumerate(range(0, count, step)):
                source = tiles.at[layer, pl.ds(first + start, step)]
                there = targets[place].at[pl.ds(start, step)]
                copies.append(pltpu.make_async_copy(source, there, semaphores.at[place, part]))
        for copy in copies:
            copy.start()
        for copy in copies:
            copy.wait()

    parts = pl.pallas_call(
        kernel,
        out_shape=[pltpu.VMEM((count, height, width), tile_weights.dtype) for _, _, count in chunks],
        in_specs=[pl.BlockSpec(memory_space=pltpu.HBM)],
        out_specs=[pl.BlockSpec(memory_space=pltpu.VMEM)] * len(chunks),
        scratch_shapes=[pltpu.SemaphoreType.DMA((len(chunks), CUTS))],
        compiler_params=pltpu.CompilerParams(vmem_limit_bytes=VMEM_LIMIT),
        cost_estimate=FREE,
    )(in_hbm(tile_weights))
    return list(parts)


def pick(table, place, number, width, activations):
    rows = activations.shape[0]

    def kernel(table, source, *refs):
        targets, semaphores = refs[:number], refs[number]
        copies = []
        for slot in range(number):
            start = pl.multiple_of(table[place + slot] * width, width)
            copies.append(pltpu.make_async_copy(source.at[:, pl.ds(start, width)], targets[slot], semaphores.at[slot]))
        for copy in copies:
            copy.start()
        for copy in copies:
            copy.wait()

    return pl.pallas_call(
        kernel,
        out_shape=[jax.ShapeDtypeStruct((rows, width), activations.dtype)] * number,
        grid_spec=pltpu.PrefetchScalarGridSpec(
            num_scalar_prefetch=1,
            in_specs=[pl.BlockSpec(memory_space=pltpu.HBM)],
            out_specs=[pl.BlockSpec(memory_space=pltpu.VMEM)] * number,
            scratch_shapes=[pltpu.SemaphoreType.DMA((number,))],
        ),
        compiler_params=pltpu.CompilerParams(vmem_limit_bytes=VMEM_LIMIT),
        cost_estimate=FREE,
    )(table, in_hbm(activations))


def run_blocks(layer, first, count, table, sends, pool, arrived, tiles, biases, target, final):
    fan, width = len(tiles), tiles[0][0].shape[2]
    rows, blocks = pool.shape[-2], biases.shape[1] // width
    columns = pool.ndim == 2
    fill = bool(arrived) and not columns
    places = {}
    for m in range(fan):
        places[m] = [(part, inside) for part, array in enumerate(tiles[m]) for inside in range(array.shape[0])]
    cuts = [block for block in range(count) if any(places[m][block][1] == 0 for m in range(fan))] + [count]
    group = math.gcd(8, *cuts)

    def kernel(*refs):
        refs = list(refs)
        table, pool_ref = (refs.pop(0) for _ in range(2))
        arrived_refs = [refs.pop(0) for _ in arrived]
        tile_refs = [[refs.pop(0) for _ in source] for source in tiles]
        bias = refs.pop(0)
        if target is not None:
            refs.pop(0)
        result = refs.pop(0)
        inputs = refs.pop(0) if fill else pool_ref
        outgoing = [] if final else [refs.pop(0) for _ in range(neigh)]
        in_sems = refs.pop(0)
        if final:
            outputs, out_sems = (refs.pop(0) for _ in range(2))
        if columns:
            inputs = refs.pop(0)

        def out_copy(part):
            here = outputs.at[:, pl.ds(part * group * width, group * width)]
            there = result.at[:, pl.ds((first + part * group) * width, group * width)]
            return pltpu.make_async_copy(here, there, out_sems.at[part])

        loads = []
        for slot, source in enumerate(arrived_refs):
            loads.append((source, inputs.at[blocks + slot]))
        if columns:
            for block in range(blocks):
                loads.append((pool_ref.at[:, pl.ds(block * width, width)], inputs.at[block]))
        loads = [pltpu.make_async_copy(*load, in_sems.at[place]) for place, load in enumerate(loads)]
        for copy in loads:
            copy.start()
        for copy in loads:
            copy.wait()

        def work(start, part, _):
            for g in range(group):
                block = part * group + g
                base = (layer * blocks + first + block) * fan
                weights = []
                for m in range(fan):
                    place, inside = places[m][start]
                    weights.append(tile_refs[m][place][block - start + inside])
                summed = jnp.dot(
                    jnp.concatenate([inputs[table[base + m]] for m in range(fan)], axis=1),
                    jnp.concatenate(weights, axis=0),
                    preferred_element_type=jnp.float32,
                )
                place = pl.multiple_of((first + block) * width, width)
                summed = summed + bias[layer : layer + 1, pl.ds(place, width)]
                summed = jnp.maximum(summed, 0.0).astype(result.dtype)
                if final:
                    outputs[:, pl.ds(pl.multiple_of(block * width, width), width)] = summed
                else:
                    result[first + block] = summed
            if final:
                out_copy(part).start()
            return _

        for start, end in zip(cuts, cuts[1:]):
            turns = (end - start) // group
            lax.fori_loop(start // group, end // group, functools.partial(work, start), None, unroll=turns if final else 1)
        for slot, there in enumerate(outgoing):
            there[...] = result[table[sends + slot]]
        if final:
            for part in range(count // group):
                out_copy(part).wait()

    anywhere = pl.BlockSpec(memory_space=pl.ANY)
    vmem, hbm = (pl.BlockSpec(memory_space=space) for space in (pltpu.VMEM, pltpu.HBM))
    neigh = NEIGH
    operands = [table, in_hbm(pool) if columns else in_vmem(pool), *arrived]
    in_specs = [hbm if columns else vmem] + [anywhere] * len(arrived)
    for source in tiles:
        operands += [in_vmem(array) for array in source]
        in_specs += [vmem] * len(source)
    operands.append(biases)
    in_specs.append(vmem)
    aliases = {}
    if target is not None:
        aliases[len(operands)] = 0
        operands.append(target)
        in_specs.append(anywhere)
    if final:
        out_shape, out_specs = [jax.ShapeDtypeStruct((rows, blocks * width), pool.dtype)], [anywhere]
    else:
        out_shape, out_specs = [pltpu.VMEM((blocks + neigh, rows, width), pool.dtype)], [vmem]
    if fill:
        aliases[1] = 1
        out_shape.append(pltpu.VMEM(pool.shape, pool.dtype))
        out_specs.append(vmem)
    if not final:
        out_shape += [jax.ShapeDtypeStruct((rows, width), pool.dtype)] * neigh
        out_specs += [vmem] * neigh
    scratch = [pltpu.SemaphoreType.DMA((len(arrived) + (blocks if columns else 0) or 1,))]
    if final:
        scratch += [pltpu.VMEM((rows, count * width), pool.dtype), pltpu.SemaphoreType.DMA((count // group,))]
    if columns:
        scratch.append(pltpu.VMEM((blocks + neigh, rows, width), pool.dtype))
    results = list(
        pl.pallas_call(
            kernel,
            out_shape=out_shape,
            grid_spec=pltpu.PrefetchScalarGridSpec(
                num_scalar_prefetch=1, in_specs=in_specs, out_specs=out_specs, scratch_shapes=scratch
            ),
            input_output_aliases=aliases,
            compiler_params=pltpu.CompilerParams(vmem_limit_bytes=LAYER_LIMIT),
            cost_estimate=FREE,
        )(*operands)
    )
    return results.pop(0), results.pop(0) if fill else pool, results


def body(activations, tile_weights, biases, source_codes, send_list):
    layer_count, block_count, part_rows, width = tile_weights.shape
    fan = source_codes.shape[2]
    part_count = lax.axis_size("dom")
    neighbor_offsets = (1, 2, -1, part_count // 2)
    sharers = width // part_rows
    own = lax.axis_index("batch") // sharers
    codes = jnp.take(source_codes, own ^ jnp.arange(fan), axis=2).reshape(-1)
    table = jnp.concatenate([codes, send_list.reshape(-1)])
    far = fan // 2
    unit = block_count // 16

    if sharers > 1:
        members = range(lax.axis_size("batch") // sharers)
        groups = [[m * sharers + s for s in range(sharers)] for m in members]
        tile_weights = lax.all_gather(tile_weights, "batch", axis=2, tiled=True, axis_index_groups=groups)

    def spread(held, first):
        for bit in range(far.bit_length() - 1):
            for m in range(1 << bit):
                held[first + m + (1 << bit)] = jax.tree.map(
                    lambda array: swapped(array, (1 << bit) * sharers), held[first + m]
                )

    last = layer_count - 1
    shares = [(layer, (8, 8), ((4, 4), (4, 4))) for layer in range(last)]
    shares += [(last, (9,), ((4, 4, 1),)), (last, (5,), ((2, 1, 1, 1),)), (last, (2,), ((2,),))]

    moves = {layer: [] for layer in range(layer_count)}
    for layer, sizes, _ in shares:
        for size in sizes:
            start = sum(count for _, _, count in moves[layer])
            moves[layer].append((layer, start, size * unit))
    mine = {layer: cut(tile_weights, moves[layer]) for layer in moves if layer}
    mine[0] = [cut(tile_weights, [move])[0] for move in moves[0]]
    crossed = {layer: [swapped(tile, far * sharers) for tile in mine[layer]] for layer in moves}

    whole = [tile_weights] + [None] * (fan - 1)
    spread(whole, 0)
    near = {layer: [cut(array, moves[layer]) for array in whole[1:far]] for layer in moves}

    current = activations
    outgoing = pick(table, codes.size, NEIGH, width, activations)
    before = None
    for layer, sizes, pieces in shares:
        if layer != before:
            arrived = [None] * NEIGH
            for turn, slot in enumerate(TURNS):
                block = outgoing[slot]
                if turn >= BOUNDARY:
                    block = lax.optimization_barrier((block, arrived[TURNS[turn - BOUNDARY]]))[0]
                arrived[slot] = shifted(block, "dom", neighbor_offsets[slot])
            pool, target, first, after = current, None, 0, arrived
        before = layer
        after = [*after, *(tile for source in near[layer] for tile in source)]
        tiles = [None] * fan
        for m, source in enumerate([mine[layer], *near[layer], crossed[layer]]):
            tiles[m] = [source.pop(0) for _ in sizes]
        for parts, tile in zip(pieces, tiles[far]):
            tile = lax.optimization_barrier((tile, *after))[0]
            passed = [None] * fan
            starts = [sum(parts[:place]) * unit for place in range(len(parts) + 1)]
            passed[far] = [tile[start:end] for start, end in zip(starts, starts[1:])]
            spread(passed, far)
            for m in range(far + 1, fan):
                tiles[m] = [*(tiles[m] or []), *passed[m]]
                after = [*after, *passed[m]]
        count = sum(sizes) * unit
        sends = codes.size + (layer + 1) * NEIGH
        target, pool, outgoing = run_blocks(
            layer, first, count, table, sends, pool, arrived, tiles, biases, target, layer == last
        )
        arrived = []
        current, first, after = target, first + count, [target]
    return current


def solution(mesh):
    in_specs = (
        P("batch", "dom"),
        P(None, "dom", "batch", None),
        P(None, "dom"),
        P(None, "dom", None),
        P(None, "dom", None),
    )
    out_specs = P("batch", "dom")
    return jax.shard_map(body, mesh=mesh, in_specs=in_specs, out_specs=out_specs, check_vma=False)
```

```python
import functools
import math

import jax
import jax.numpy as jnp
from jax import lax
from jax.experimental import pallas as pl
from jax.experimental.pallas import tpu as pltpu
from jax.sharding import PartitionSpec as P

TURNS = (3, 1, 0, 2)
BOUNDARY = 2
CUTS = 16
NEIGH = 4
VMEM_LIMIT = 16 * 2**20
LAYER_LIMIT = 20 * 2**20
FREE = pl.CostEstimate(flops=0, bytes_accessed=0, transcendentals=0)


def shifted(block, axis, distance):
    devices = range(lax.axis_size(axis))
    route = [((i - distance) % len(devices), i) for i in devices]
    return lax.ppermute(block, axis, route)


def swapped(block, mask):
    route = [(i, i ^ mask) for i in range(lax.axis_size("batch"))]
    return lax.ppermute(block, "batch", route)


def in_hbm(array):
    return pltpu.with_memory_space_constraint(array, pltpu.HBM)


def in_vmem(array):
    return pltpu.with_memory_space_constraint(array, pltpu.VMEM)


def cut(tile_weights, chunks):
    height, width = tile_weights.shape[2:]

    def kernel(tiles, *refs):
        targets, semaphores = refs[: len(chunks)], refs[len(chunks)]
        copies = []
        for place, (layer, first, count) in enumerate(chunks):
            step = count // math.gcd(CUTS, count)
            for part, start in enumerate(range(0, count, step)):
                source = tiles.at[layer, pl.ds(first + start, step)]
                there = targets[place].at[pl.ds(start, step)]
                copies.append(pltpu.make_async_copy(source, there, semaphores.at[place, part]))
        for copy in copies:
            copy.start()
        for copy in copies:
            copy.wait()

    parts = pl.pallas_call(
        kernel,
        out_shape=[pltpu.VMEM((count, height, width), tile_weights.dtype) for _, _, count in chunks],
        in_specs=[pl.BlockSpec(memory_space=pltpu.HBM)],
        out_specs=[pl.BlockSpec(memory_space=pltpu.VMEM)] * len(chunks),
        scratch_shapes=[pltpu.SemaphoreType.DMA((len(chunks), CUTS))],
        compiler_params=pltpu.CompilerParams(vmem_limit_bytes=VMEM_LIMIT),
        cost_estimate=FREE,
    )(in_hbm(tile_weights))
    return list(parts)


def pick(table, place, number, width, activations):
    rows = activations.shape[0]

    def kernel(table, source, *refs):
        targets, semaphores = refs[:number], refs[number]
        copies = []
        for slot in range(number):
            start = pl.multiple_of(table[place + slot] * width, width)
            copies.append(pltpu.make_async_copy(source.at[:, pl.ds(start, width)], targets[slot], semaphores.at[slot]))
        for copy in copies:
            copy.start()
        for copy in copies:
            copy.wait()

    return pl.pallas_call(
        kernel,
        out_shape=[jax.ShapeDtypeStruct((rows, width), activations.dtype)] * number,
        grid_spec=pltpu.PrefetchScalarGridSpec(
            num_scalar_prefetch=1,
            in_specs=[pl.BlockSpec(memory_space=pltpu.HBM)],
            out_specs=[pl.BlockSpec(memory_space=pltpu.VMEM)] * number,
            scratch_shapes=[pltpu.SemaphoreType.DMA((number,))],
        ),
        compiler_params=pltpu.CompilerParams(vmem_limit_bytes=VMEM_LIMIT),
        cost_estimate=FREE,
    )(table, in_hbm(activations))


def run_blocks(layer, first, count, table, sends, pool, arrived, tiles, biases, target, final):
    fan, width = len(tiles), tiles[0][0].shape[2]
    rows, blocks = pool.shape[-2], biases.shape[1] // width
    columns = pool.ndim == 2
    fill = bool(arrived) and not columns
    places = {}
    for m in range(fan):
        places[m] = [(part, inside) for part, array in enumerate(tiles[m]) for inside in range(array.shape[0])]
    cuts = [block for block in range(count) if any(places[m][block][1] == 0 for m in range(fan))] + [count]
    group = math.gcd(2 if final else 8, *cuts)

    def kernel(*refs):
        refs = list(refs)
        table, pool_ref = (refs.pop(0) for _ in range(2))
        arrived_refs = [refs.pop(0) for _ in arrived]
        tile_refs = [[refs.pop(0) for _ in source] for source in tiles]
        bias = refs.pop(0)
        if target is not None:
            refs.pop(0)
        result = refs.pop(0)
        inputs = refs.pop(0) if fill else pool_ref
        outgoing = [] if final else [refs.pop(0) for _ in range(neigh)]
        in_sems = refs.pop(0)
        if final:
            outputs, out_sems = (refs.pop(0) for _ in range(2))
        if columns:
            inputs = refs.pop(0)

        def out_copy(part):
            here = outputs.at[:, pl.ds(part * group * width, group * width)]
            there = result.at[:, pl.ds((first + part * group) * width, group * width)]
            return pltpu.make_async_copy(here, there, out_sems.at[part])

        loads = []
        for slot, source in enumerate(arrived_refs):
            loads.append((source, inputs.at[blocks + slot]))
        if columns:
            for block in range(blocks):
                loads.append((pool_ref.at[:, pl.ds(block * width, width)], inputs.at[block]))
        loads = [pltpu.make_async_copy(*load, in_sems.at[place]) for place, load in enumerate(loads)]
        for copy in loads:
            copy.start()
        for copy in loads:
            copy.wait()

        def work(start, part, _):
            for g in range(group):
                block = part * group + g
                base = (layer * blocks + first + block) * fan
                weights = []
                for m in range(fan):
                    place, inside = places[m][start]
                    weights.append(tile_refs[m][place][block - start + inside])
                summed = jnp.dot(
                    jnp.concatenate([inputs[table[base + m]] for m in range(fan)], axis=1),
                    jnp.concatenate(weights, axis=0),
                    preferred_element_type=jnp.float32,
                )
                place = pl.multiple_of((first + block) * width, width)
                summed = summed + bias[layer : layer + 1, pl.ds(place, width)]
                summed = jnp.maximum(summed, 0.0).astype(result.dtype)
                if final:
                    outputs[:, pl.ds(pl.multiple_of(block * width, width), width)] = summed
                else:
                    result[first + block] = summed
            if final:
                out_copy(part).start()
            return _

        for start, end in zip(cuts, cuts[1:]):
            turns = (end - start) // group
            lax.fori_loop(start // group, end // group, functools.partial(work, start), None, unroll=turns if final else 1)
        for slot, there in enumerate(outgoing):
            there[...] = result[table[sends + slot]]
        if final:
            for part in range(count // group):
                out_copy(part).wait()

    anywhere = pl.BlockSpec(memory_space=pl.ANY)
    vmem, hbm = (pl.BlockSpec(memory_space=space) for space in (pltpu.VMEM, pltpu.HBM))
    neigh = NEIGH
    operands = [table, in_hbm(pool) if columns else in_vmem(pool), *arrived]
    in_specs = [hbm if columns else vmem] + [anywhere] * len(arrived)
    for source in tiles:
        operands += [in_vmem(array) for array in source]
        in_specs += [vmem] * len(source)
    operands.append(biases)
    in_specs.append(vmem)
    aliases = {}
    if target is not None:
        aliases[len(operands)] = 0
        operands.append(target)
        in_specs.append(anywhere)
    if final:
        out_shape, out_specs = [jax.ShapeDtypeStruct((rows, blocks * width), pool.dtype)], [anywhere]
    else:
        out_shape, out_specs = [pltpu.VMEM((blocks + neigh, rows, width), pool.dtype)], [vmem]
    if fill:
        aliases[1] = 1
        out_shape.append(pltpu.VMEM(pool.shape, pool.dtype))
        out_specs.append(vmem)
    if not final:
        out_shape += [jax.ShapeDtypeStruct((rows, width), pool.dtype)] * neigh
        out_specs += [vmem] * neigh
    scratch = [pltpu.SemaphoreType.DMA((len(arrived) + (blocks if columns else 0) or 1,))]
    if final:
        scratch += [pltpu.VMEM((rows, count * width), pool.dtype), pltpu.SemaphoreType.DMA((count // group,))]
    if columns:
        scratch.append(pltpu.VMEM((blocks + neigh, rows, width), pool.dtype))
    results = list(
        pl.pallas_call(
            kernel,
            out_shape=out_shape,
            grid_spec=pltpu.PrefetchScalarGridSpec(
                num_scalar_prefetch=1, in_specs=in_specs, out_specs=out_specs, scratch_shapes=scratch
            ),
            input_output_aliases=aliases,
            compiler_params=pltpu.CompilerParams(vmem_limit_bytes=LAYER_LIMIT),
            cost_estimate=FREE,
        )(*operands)
    )
    return results.pop(0), results.pop(0) if fill else pool, results


def body(activations, tile_weights, biases, source_codes, send_list):
    layer_count, block_count, part_rows, width = tile_weights.shape
    fan = source_codes.shape[2]
    part_count = lax.axis_size("dom")
    neighbor_offsets = (1, 2, -1, part_count // 2)
    sharers = width // part_rows
    own = lax.axis_index("batch") // sharers
    codes = jnp.take(source_codes, own ^ jnp.arange(fan), axis=2).reshape(-1)
    table = jnp.concatenate([codes, send_list.reshape(-1)])
    far = fan // 2
    unit = block_count // 16

    if sharers > 1:
        members = range(lax.axis_size("batch") // sharers)
        groups = [[m * sharers + s for s in range(sharers)] for m in members]
        tile_weights = lax.all_gather(tile_weights, "batch", axis=2, tiled=True, axis_index_groups=groups)

    def spread(held, first):
        for bit in range(far.bit_length() - 1):
            for m in range(1 << bit):
                held[first + m + (1 << bit)] = jax.tree.map(
                    lambda array: swapped(array, (1 << bit) * sharers), held[first + m]
                )

    last = layer_count - 1
    shares = [(layer, (8, 8), ((4, 4), (4, 4))) for layer in range(last)]
    shares += [(last, (9,), ((4, 4, 1),)), (last, (5,), ((2, 1, 1, 1),)), (last, (2,), ((2,),))]

    moves = {layer: [] for layer in range(layer_count)}
    for layer, sizes, _ in shares:
        for size in sizes:
            start = sum(count for _, _, count in moves[layer])
            moves[layer].append((layer, start, size * unit))
    mine = {layer: cut(tile_weights, moves[layer]) for layer in moves if layer}
    mine[0] = [cut(tile_weights, [move])[0] for move in moves[0]]
    crossed = {layer: [swapped(tile, far * sharers) for tile in mine[layer]] for layer in moves}

    whole = [tile_weights] + [None] * (fan - 1)
    spread(whole, 0)
    near = {layer: [cut(array, moves[layer]) for array in whole[1:far]] for layer in moves}

    current = activations
    outgoing = pick(table, codes.size, NEIGH, width, activations)
    before = None
    for layer, sizes, pieces in shares:
        if layer != before:
            arrived = [None] * NEIGH
            for turn, slot in enumerate(TURNS):
                block = outgoing[slot]
                if turn >= BOUNDARY:
                    block = lax.optimization_barrier((block, arrived[TURNS[turn - BOUNDARY]]))[0]
                arrived[slot] = shifted(block, "dom", neighbor_offsets[slot])
            pool, target, first, after = current, None, 0, arrived
        before = layer
        after = [*after, *(tile for source in near[layer] for tile in source)]
        tiles = [None] * fan
        for m, source in enumerate([mine[layer], *near[layer], crossed[layer]]):
            tiles[m] = [source.pop(0) for _ in sizes]
        for parts, tile in zip(pieces, tiles[far]):
            tile = lax.optimization_barrier((tile, *after))[0]
            passed = [None] * fan
            starts = [sum(parts[:place]) * unit for place in range(len(parts) + 1)]
            passed[far] = [tile[start:end] for start, end in zip(starts, starts[1:])]
            spread(passed, far)
            for m in range(far + 1, fan):
                tiles[m] = [*(tiles[m] or []), *passed[m]]
                after = [*after, *passed[m]]
        count = sum(sizes) * unit
        sends = codes.size + (layer + 1) * NEIGH
        target, pool, outgoing = run_blocks(
            layer, first, count, table, sends, pool, arrived, tiles, biases, target, layer == last
        )
        arrived = []
        current, first, after = target, first + count, [target]
    return current


def solution(mesh):
    in_specs = (
        P("batch", "dom"),
        P(None, "dom", "batch", None),
        P(None, "dom"),
        P(None, "dom", None),
        P(None, "dom", None),
    )
    out_specs = P("batch", "dom")
    return jax.shard_map(body, mesh=mesh, in_specs=in_specs, out_specs=out_specs, check_vma=False)
```

```python
import functools
import math

import jax
import jax.numpy as jnp
from jax import lax
from jax.experimental import pallas as pl
from jax.experimental.pallas import tpu as pltpu
from jax.sharding import PartitionSpec as P

TURNS = (3, 1, 0, 2)
BOUNDARY = 2
CUTS = 8
NEIGH = 4
VMEM_LIMIT = 16 * 2**20
LAYER_LIMIT = 20 * 2**20
FREE = pl.CostEstimate(flops=0, bytes_accessed=0, transcendentals=0)


def shifted(block, axis, distance):
    devices = range(lax.axis_size(axis))
    route = [((i - distance) % len(devices), i) for i in devices]
    return lax.ppermute(block, axis, route)


def swapped(block, mask):
    route = [(i, i ^ mask) for i in range(lax.axis_size("batch"))]
    return lax.ppermute(block, "batch", route)


def in_hbm(array):
    return pltpu.with_memory_space_constraint(array, pltpu.HBM)


def in_vmem(array):
    return pltpu.with_memory_space_constraint(array, pltpu.VMEM)


def cut(tile_weights, chunks):
    height, width = tile_weights.shape[2:]

    def kernel(tiles, *refs):
        targets, semaphores = refs[: len(chunks)], refs[len(chunks)]
        copies = []
        for place, (layer, first, count) in enumerate(chunks):
            step = count // math.gcd(CUTS, count)
            for part, start in enumerate(range(0, count, step)):
                source = tiles.at[layer, pl.ds(first + start, step)]
                there = targets[place].at[pl.ds(start, step)]
                copies.append(pltpu.make_async_copy(source, there, semaphores.at[place, part]))
        for copy in copies:
            copy.start()
        for copy in copies:
            copy.wait()

    parts = pl.pallas_call(
        kernel,
        out_shape=[pltpu.VMEM((count, height, width), tile_weights.dtype) for _, _, count in chunks],
        in_specs=[pl.BlockSpec(memory_space=pltpu.HBM)],
        out_specs=[pl.BlockSpec(memory_space=pltpu.VMEM)] * len(chunks),
        scratch_shapes=[pltpu.SemaphoreType.DMA((len(chunks), CUTS))],
        compiler_params=pltpu.CompilerParams(vmem_limit_bytes=VMEM_LIMIT),
        cost_estimate=FREE,
    )(in_hbm(tile_weights))
    return list(parts)


def pick(table, place, number, width, activations):
    rows = activations.shape[0]

    def kernel(table, source, *refs):
        targets, semaphores = refs[:number], refs[number]
        copies = []
        for slot in range(number):
            start = pl.multiple_of(table[place + slot] * width, width)
            copies.append(pltpu.make_async_copy(source.at[:, pl.ds(start, width)], targets[slot], semaphores.at[slot]))
        for copy in copies:
            copy.start()
        for copy in copies:
            copy.wait()

    return pl.pallas_call(
        kernel,
        out_shape=[jax.ShapeDtypeStruct((rows, width), activations.dtype)] * number,
        grid_spec=pltpu.PrefetchScalarGridSpec(
            num_scalar_prefetch=1,
            in_specs=[pl.BlockSpec(memory_space=pltpu.HBM)],
            out_specs=[pl.BlockSpec(memory_space=pltpu.VMEM)] * number,
            scratch_shapes=[pltpu.SemaphoreType.DMA((number,))],
        ),
        compiler_params=pltpu.CompilerParams(vmem_limit_bytes=VMEM_LIMIT),
        cost_estimate=FREE,
    )(table, in_hbm(activations))


def run_blocks(layer, first, count, table, sends, pool, arrived, tiles, biases, target, final):
    fan, width = len(tiles), tiles[0][0].shape[2]
    rows, blocks = pool.shape[-2], biases.shape[1] // width
    columns = pool.ndim == 2
    fill = bool(arrived) and not columns
    places = {}
    for m in range(fan):
        places[m] = [(part, inside) for part, array in enumerate(tiles[m]) for inside in range(array.shape[0])]
    cuts = [block for block in range(count) if any(places[m][block][1] == 0 for m in range(fan))] + [count]
    group = math.gcd(2 if final else 8, *cuts)

    def kernel(*refs):
        refs = list(refs)
        table, pool_ref = (refs.pop(0) for _ in range(2))
        arrived_refs = [refs.pop(0) for _ in arrived]
        tile_refs = [[refs.pop(0) for _ in source] for source in tiles]
        bias = refs.pop(0)
        if target is not None:
            refs.pop(0)
        result = refs.pop(0)
        inputs = refs.pop(0) if fill else pool_ref
        outgoing = [] if final else [refs.pop(0) for _ in range(neigh)]
        in_sems = refs.pop(0)
        if final:
            outputs, out_sems = (refs.pop(0) for _ in range(2))
        if columns:
            inputs = refs.pop(0)

        def out_copy(part):
            here = outputs.at[:, pl.ds(part * group * width, group * width)]
            there = result.at[:, pl.ds((first + part * group) * width, group * width)]
            return pltpu.make_async_copy(here, there, out_sems.at[part])

        loads = []
        for slot, source in enumerate(arrived_refs):
            loads.append((source, inputs.at[blocks + slot]))
        if columns:
            for block in range(blocks):
                loads.append((pool_ref.at[:, pl.ds(block * width, width)], inputs.at[block]))
        loads = [pltpu.make_async_copy(*load, in_sems.at[place]) for place, load in enumerate(loads)]
        for copy in loads:
            copy.start()
        for copy in loads:
            copy.wait()

        def work(start, part, _):
            for g in range(group):
                block = part * group + g
                base = (layer * blocks + first + block) * fan
                weights = []
                for m in range(fan):
                    place, inside = places[m][start]
                    weights.append(tile_refs[m][place][block - start + inside])
                summed = jnp.dot(
                    jnp.concatenate([inputs[table[base + m]] for m in range(fan)], axis=1),
                    jnp.concatenate(weights, axis=0),
                    preferred_element_type=jnp.float32,
                )
                place = pl.multiple_of((first + block) * width, width)
                summed = summed + bias[layer : layer + 1, pl.ds(place, width)]
                summed = jnp.maximum(summed, 0.0).astype(result.dtype)
                if final:
                    outputs[:, pl.ds(pl.multiple_of(block * width, width), width)] = summed
                else:
                    result[first + block] = summed
            if final:
                out_copy(part).start()
            return _

        for start, end in zip(cuts, cuts[1:]):
            turns = (end - start) // group
            lax.fori_loop(start // group, end // group, functools.partial(work, start), None, unroll=turns if final else 1)
        for slot, there in enumerate(outgoing):
            there[...] = result[table[sends + slot]]
        if final:
            for part in range(count // group):
                out_copy(part).wait()

    anywhere = pl.BlockSpec(memory_space=pl.ANY)
    vmem, hbm = (pl.BlockSpec(memory_space=space) for space in (pltpu.VMEM, pltpu.HBM))
    neigh = NEIGH
    operands = [table, in_hbm(pool) if columns else in_vmem(pool), *arrived]
    in_specs = [hbm if columns else vmem] + [anywhere] * len(arrived)
    for source in tiles:
        operands += [in_vmem(array) for array in source]
        in_specs += [vmem] * len(source)
    operands.append(biases)
    in_specs.append(vmem)
    aliases = {}
    if target is not None:
        aliases[len(operands)] = 0
        operands.append(target)
        in_specs.append(anywhere)
    if final:
        out_shape, out_specs = [jax.ShapeDtypeStruct((rows, blocks * width), pool.dtype)], [anywhere]
    else:
        out_shape, out_specs = [pltpu.VMEM((blocks + neigh, rows, width), pool.dtype)], [vmem]
    if fill:
        aliases[1] = 1
        out_shape.append(pltpu.VMEM(pool.shape, pool.dtype))
        out_specs.append(vmem)
    if not final:
        out_shape += [jax.ShapeDtypeStruct((rows, width), pool.dtype)] * neigh
        out_specs += [vmem] * neigh
    scratch = [pltpu.SemaphoreType.DMA((len(arrived) + (blocks if columns else 0) or 1,))]
    if final:
        scratch += [pltpu.VMEM((rows, count * width), pool.dtype), pltpu.SemaphoreType.DMA((count // group,))]
    if columns:
        scratch.append(pltpu.VMEM((blocks + neigh, rows, width), pool.dtype))
    results = list(
        pl.pallas_call(
            kernel,
            out_shape=out_shape,
            grid_spec=pltpu.PrefetchScalarGridSpec(
                num_scalar_prefetch=1, in_specs=in_specs, out_specs=out_specs, scratch_shapes=scratch
            ),
            input_output_aliases=aliases,
            compiler_params=pltpu.CompilerParams(vmem_limit_bytes=LAYER_LIMIT),
            cost_estimate=FREE,
        )(*operands)
    )
    return results.pop(0), results.pop(0) if fill else pool, results


def body(activations, tile_weights, biases, source_codes, send_list):
    layer_count, block_count, part_rows, width = tile_weights.shape
    fan = source_codes.shape[2]
    part_count = lax.axis_size("dom")
    neighbor_offsets = (1, 2, -1, part_count // 2)
    sharers = width // part_rows
    own = lax.axis_index("batch") // sharers
    codes = jnp.take(source_codes, own ^ jnp.arange(fan), axis=2).reshape(-1)
    table = jnp.concatenate([codes, send_list.reshape(-1)])
    far = fan // 2
    unit = block_count // 16

    if sharers > 1:
        members = range(lax.axis_size("batch") // sharers)
        groups = [[m * sharers + s for s in range(sharers)] for m in members]
        tile_weights = lax.all_gather(tile_weights, "batch", axis=2, tiled=True, axis_index_groups=groups)

    def spread(held, first):
        for bit in range(far.bit_length() - 1):
            for m in range(1 << bit):
                held[first + m + (1 << bit)] = jax.tree.map(
                    lambda array: swapped(array, (1 << bit) * sharers), held[first + m]
                )

    last = layer_count - 1
    shares = [(layer, (8, 8), ((4, 4), (4, 4))) for layer in range(last)]
    shares += [(last, (9,), ((4, 4, 1),)), (last, (5,), ((2, 1, 1, 1),)), (last, (2,), ((2,),))]

    moves = {layer: [] for layer in range(layer_count)}
    for layer, sizes, _ in shares:
        for size in sizes:
            start = sum(count for _, _, count in moves[layer])
            moves[layer].append((layer, start, size * unit))
    mine = {layer: cut(tile_weights, moves[layer]) for layer in moves if layer}
    mine[0] = [cut(tile_weights, [move])[0] for move in moves[0]]
    crossed = {layer: [swapped(tile, far * sharers) for tile in mine[layer]] for layer in moves}

    whole = [tile_weights] + [None] * (fan - 1)
    spread(whole, 0)
    near = {layer: [cut(array, moves[layer]) for array in whole[1:far]] for layer in moves}

    current = activations
    outgoing = pick(table, codes.size, NEIGH, width, activations)
    before = None
    for layer, sizes, pieces in shares:
        if layer != before:
            arrived = [None] * NEIGH
            for turn, slot in enumerate(TURNS):
                block = outgoing[slot]
                if turn >= BOUNDARY:
                    block = lax.optimization_barrier((block, arrived[TURNS[turn - BOUNDARY]]))[0]
                arrived[slot] = shifted(block, "dom", neighbor_offsets[slot])
            pool, target, first, after = current, None, 0, arrived
        before = layer
        after = [*after, *(tile for source in near[layer] for tile in source)]
        tiles = [None] * fan
        for m, source in enumerate([mine[layer], *near[layer], crossed[layer]]):
            tiles[m] = [source.pop(0) for _ in sizes]
        for parts, tile in zip(pieces, tiles[far]):
            tile = lax.optimization_barrier((tile, *after))[0]
            passed = [None] * fan
            starts = [sum(parts[:place]) * unit for place in range(len(parts) + 1)]
            passed[far] = [tile[start:end] for start, end in zip(starts, starts[1:])]
            spread(passed, far)
            for m in range(far + 1, fan):
                tiles[m] = [*(tiles[m] or []), *passed[m]]
                after = [*after, *passed[m]]
        count = sum(sizes) * unit
        sends = codes.size + (layer + 1) * NEIGH
        target, pool, outgoing = run_blocks(
            layer, first, count, table, sends, pool, arrived, tiles, biases, target, layer == last
        )
        arrived = []
        current, first, after = target, first + count, [target]
    return current


def solution(mesh):
    in_specs = (
        P("batch", "dom"),
        P(None, "dom", "batch", None),
        P(None, "dom"),
        P(None, "dom", None),
        P(None, "dom", None),
    )
    out_specs = P("batch", "dom")
    return jax.shard_map(body, mesh=mesh, in_specs=in_specs, out_specs=out_specs, check_vma=False)
```

```python
import functools
import math

import jax
import jax.numpy as jnp
from jax import lax
from jax.experimental import pallas as pl
from jax.experimental.pallas import tpu as pltpu
from jax.sharding import PartitionSpec as P

TURNS = (3, 1, 0, 2)
BOUNDARY = 2
CUTS = 8
NEIGH = 4
VMEM_LIMIT = 16 * 2**20
LAYER_LIMIT = 20 * 2**20
FREE = pl.CostEstimate(flops=0, bytes_accessed=0, transcendentals=0)


def shifted(block, axis, distance):
    devices = range(lax.axis_size(axis))
    route = [((i - distance) % len(devices), i) for i in devices]
    return lax.ppermute(block, axis, route)


def swapped(block, mask):
    route = [(i, i ^ mask) for i in range(lax.axis_size("batch"))]
    return lax.ppermute(block, "batch", route)


def in_hbm(array):
    return pltpu.with_memory_space_constraint(array, pltpu.HBM)


def in_vmem(array):
    return pltpu.with_memory_space_constraint(array, pltpu.VMEM)


def cut(tile_weights, chunks):
    height, width = tile_weights.shape[2:]

    def kernel(tiles, *refs):
        targets, semaphores = refs[: len(chunks)], refs[len(chunks)]
        copies = []
        for place, (layer, first, count) in enumerate(chunks):
            step = count // math.gcd(CUTS, count)
            for part, start in enumerate(range(0, count, step)):
                source = tiles.at[layer, pl.ds(first + start, step)]
                there = targets[place].at[pl.ds(start, step)]
                copies.append(pltpu.make_async_copy(source, there, semaphores.at[place, part]))
        for copy in copies:
            copy.start()
        for copy in copies:
            copy.wait()

    parts = pl.pallas_call(
        kernel,
        out_shape=[pltpu.VMEM((count, height, width), tile_weights.dtype) for _, _, count in chunks],
        in_specs=[pl.BlockSpec(memory_space=pltpu.HBM)],
        out_specs=[pl.BlockSpec(memory_space=pltpu.VMEM)] * len(chunks),
        scratch_shapes=[pltpu.SemaphoreType.DMA((len(chunks), CUTS))],
        compiler_params=pltpu.CompilerParams(vmem_limit_bytes=VMEM_LIMIT),
        cost_estimate=FREE,
    )(in_hbm(tile_weights))
    return list(parts)


def pick(table, place, number, width, activations):
    rows = activations.shape[0]

    def kernel(table, source, *refs):
        targets, semaphores = refs[:number], refs[number]
        copies = []
        for slot in range(number):
            start = pl.multiple_of(table[place + slot] * width, width)
            copies.append(pltpu.make_async_copy(source.at[:, pl.ds(start, width)], targets[slot], semaphores.at[slot]))
        for copy in copies:
            copy.start()
        for copy in copies:
            copy.wait()

    return pl.pallas_call(
        kernel,
        out_shape=[jax.ShapeDtypeStruct((rows, width), activations.dtype)] * number,
        grid_spec=pltpu.PrefetchScalarGridSpec(
            num_scalar_prefetch=1,
            in_specs=[pl.BlockSpec(memory_space=pltpu.HBM)],
            out_specs=[pl.BlockSpec(memory_space=pltpu.VMEM)] * number,
            scratch_shapes=[pltpu.SemaphoreType.DMA((number,))],
        ),
        compiler_params=pltpu.CompilerParams(vmem_limit_bytes=VMEM_LIMIT),
        cost_estimate=FREE,
    )(table, in_hbm(activations))


def run_blocks(layer, first, count, table, sends, pool, arrived, tiles, biases, target, final):
    fan, width = len(tiles), tiles[0][0].shape[2]
    rows, blocks = pool.shape[-2], biases.shape[1] // width
    columns = pool.ndim == 2
    fill = bool(arrived) and not columns
    places = {}
    for m in range(fan):
        places[m] = [(part, inside) for part, array in enumerate(tiles[m]) for inside in range(array.shape[0])]
    cuts = [block for block in range(count) if any(places[m][block][1] == 0 for m in range(fan))] + [count]
    group = math.gcd(2 if final else 8, *cuts)

    def kernel(*refs):
        refs = list(refs)
        table, pool_ref = (refs.pop(0) for _ in range(2))
        arrived_refs = [refs.pop(0) for _ in arrived]
        tile_refs = [[refs.pop(0) for _ in source] for source in tiles]
        bias = refs.pop(0)
        if target is not None:
            refs.pop(0)
        result = refs.pop(0)
        inputs = refs.pop(0) if fill else pool_ref
        outgoing = [] if final else [refs.pop(0) for _ in range(neigh)]
        in_sems = refs.pop(0)
        if final:
            outputs, out_sems = (refs.pop(0) for _ in range(2))
        if columns:
            inputs = refs.pop(0)

        def out_copy(part):
            here = outputs.at[:, pl.ds(part * group * width, group * width)]
            there = result.at[:, pl.ds((first + part * group) * width, group * width)]
            return pltpu.make_async_copy(here, there, out_sems.at[part])

        loads = []
        for slot, source in enumerate(arrived_refs):
            loads.append((source, inputs.at[blocks + slot]))
        if columns:
            for block in range(blocks):
                loads.append((pool_ref.at[:, pl.ds(block * width, width)], inputs.at[block]))
        loads = [pltpu.make_async_copy(*load, in_sems.at[place]) for place, load in enumerate(loads)]
        for copy in loads:
            copy.start()
        for copy in loads:
            copy.wait()

        def work(start, part, _):
            for g in range(group):
                block = part * group + g
                base = (layer * blocks + first + block) * fan
                weights = []
                for m in range(fan):
                    place, inside = places[m][start]
                    weights.append(tile_refs[m][place][block - start + inside])
                panel = [inputs[table[base + m]] for m in range(fan)]
                halves = [
                    jnp.dot(
                        jnp.concatenate(panel[half], axis=1),
                        jnp.concatenate(weights[half], axis=0),
                        preferred_element_type=jnp.float32,
                    )
                    for half in (slice(0, fan // 2), slice(fan // 2, fan))
                ]
                summed = halves[0] + halves[1]
                place = pl.multiple_of((first + block) * width, width)
                summed = summed + bias[layer : layer + 1, pl.ds(place, width)]
                summed = jnp.maximum(summed, 0.0).astype(result.dtype)
                if final:
                    outputs[:, pl.ds(pl.multiple_of(block * width, width), width)] = summed
                else:
                    result[first + block] = summed
            if final:
                out_copy(part).start()
            return _

        for start, end in zip(cuts, cuts[1:]):
            turns = (end - start) // group
            lax.fori_loop(start // group, end // group, functools.partial(work, start), None, unroll=turns if final else 1)
        for slot, there in enumerate(outgoing):
            there[...] = result[table[sends + slot]]
        if final:
            for part in range(count // group):
                out_copy(part).wait()

    anywhere = pl.BlockSpec(memory_space=pl.ANY)
    vmem, hbm = (pl.BlockSpec(memory_space=space) for space in (pltpu.VMEM, pltpu.HBM))
    neigh = NEIGH
    operands = [table, in_hbm(pool) if columns else in_vmem(pool), *arrived]
    in_specs = [hbm if columns else vmem] + [anywhere] * len(arrived)
    for source in tiles:
        operands += [in_vmem(array) for array in source]
        in_specs += [vmem] * len(source)
    operands.append(biases)
    in_specs.append(vmem)
    aliases = {}
    if target is not None:
        aliases[len(operands)] = 0
        operands.append(target)
        in_specs.append(anywhere)
    if final:
        out_shape, out_specs = [jax.ShapeDtypeStruct((rows, blocks * width), pool.dtype)], [anywhere]
    else:
        out_shape, out_specs = [pltpu.VMEM((blocks + neigh, rows, width), pool.dtype)], [vmem]
    if fill:
        aliases[1] = 1
        out_shape.append(pltpu.VMEM(pool.shape, pool.dtype))
        out_specs.append(vmem)
    if not final:
        out_shape += [jax.ShapeDtypeStruct((rows, width), pool.dtype)] * neigh
        out_specs += [vmem] * neigh
    scratch = [pltpu.SemaphoreType.DMA((len(arrived) + (blocks if columns else 0) or 1,))]
    if final:
        scratch += [pltpu.VMEM((rows, count * width), pool.dtype), pltpu.SemaphoreType.DMA((count // group,))]
    if columns:
        scratch.append(pltpu.VMEM((blocks + neigh, rows, width), pool.dtype))
    results = list(
        pl.pallas_call(
            kernel,
            out_shape=out_shape,
            grid_spec=pltpu.PrefetchScalarGridSpec(
                num_scalar_prefetch=1, in_specs=in_specs, out_specs=out_specs, scratch_shapes=scratch
            ),
            input_output_aliases=aliases,
            compiler_params=pltpu.CompilerParams(vmem_limit_bytes=LAYER_LIMIT),
            cost_estimate=FREE,
        )(*operands)
    )
    return results.pop(0), results.pop(0) if fill else pool, results


def body(activations, tile_weights, biases, source_codes, send_list):
    layer_count, block_count, part_rows, width = tile_weights.shape
    fan = source_codes.shape[2]
    part_count = lax.axis_size("dom")
    neighbor_offsets = (1, 2, -1, part_count // 2)
    sharers = width // part_rows
    own = lax.axis_index("batch") // sharers
    codes = jnp.take(source_codes, own ^ jnp.arange(fan), axis=2).reshape(-1)
    table = jnp.concatenate([codes, send_list.reshape(-1)])
    far = fan // 2
    unit = block_count // 16

    if sharers > 1:
        members = range(lax.axis_size("batch") // sharers)
        groups = [[m * sharers + s for s in range(sharers)] for m in members]
        tile_weights = lax.all_gather(tile_weights, "batch", axis=2, tiled=True, axis_index_groups=groups)

    def spread(held, first):
        for bit in range(far.bit_length() - 1):
            for m in range(1 << bit):
                held[first + m + (1 << bit)] = jax.tree.map(
                    lambda array: swapped(array, (1 << bit) * sharers), held[first + m]
                )

    last = layer_count - 1
    shares = [(layer, (8, 8), ((4, 4), (4, 4))) for layer in range(last)]
    shares += [(last, (9,), ((4, 4, 1),)), (last, (5,), ((2, 1, 1, 1),)), (last, (2,), ((2,),))]

    moves = {layer: [] for layer in range(layer_count)}
    for layer, sizes, _ in shares:
        for size in sizes:
            start = sum(count for _, _, count in moves[layer])
            moves[layer].append((layer, start, size * unit))
    mine = {layer: cut(tile_weights, moves[layer]) for layer in moves if layer}
    mine[0] = [cut(tile_weights, [move])[0] for move in moves[0]]
    crossed = {layer: [swapped(tile, far * sharers) for tile in mine[layer]] for layer in moves}

    whole = [tile_weights] + [None] * (fan - 1)
    spread(whole, 0)
    near = {layer: [cut(array, moves[layer]) for array in whole[1:far]] for layer in moves}

    current = activations
    outgoing = pick(table, codes.size, NEIGH, width, activations)
    before = None
    for layer, sizes, pieces in shares:
        if layer != before:
            arrived = [None] * NEIGH
            for turn, slot in enumerate(TURNS):
                block = outgoing[slot]
                if turn >= BOUNDARY:
                    block = lax.optimization_barrier((block, arrived[TURNS[turn - BOUNDARY]]))[0]
                arrived[slot] = shifted(block, "dom", neighbor_offsets[slot])
            pool, target, first, after = current, None, 0, arrived
        before = layer
        after = [*after, *(tile for source in near[layer] for tile in source)]
        tiles = [None] * fan
        for m, source in enumerate([mine[layer], *near[layer], crossed[layer]]):
            tiles[m] = [source.pop(0) for _ in sizes]
        for parts, tile in zip(pieces, tiles[far]):
            tile = lax.optimization_barrier((tile, *after))[0]
            passed = [None] * fan
            starts = [sum(parts[:place]) * unit for place in range(len(parts) + 1)]
            passed[far] = [tile[start:end] for start, end in zip(starts, starts[1:])]
            spread(passed, far)
            for m in range(far + 1, fan):
                tiles[m] = [*(tiles[m] or []), *passed[m]]
                after = [*after, *passed[m]]
        count = sum(sizes) * unit
        sends = codes.size + (layer + 1) * NEIGH
        target, pool, outgoing = run_blocks(
            layer, first, count, table, sends, pool, arrived, tiles, biases, target, layer == last
        )
        arrived = []
        current, first, after = target, first + count, [target]
    return current


def solution(mesh):
    in_specs = (
        P("batch", "dom"),
        P(None, "dom", "batch", None),
        P(None, "dom"),
        P(None, "dom", None),
        P(None, "dom", None),
    )
    out_specs = P("batch", "dom")
    return jax.shard_map(body, mesh=mesh, in_specs=in_specs, out_specs=out_specs, check_vma=False)
```
